512 devices in a mesh: slab: 64 (over z, x), tile: 8 (over y, core).
Axes of the slice: x: 4, y: 4, z: 16, core: 2. Of those that a mesh axis runs over, the one named last changes fastest.
Arguments:
- images: float32 [256, 2048, 256], P('slab', 'tile'), may hold values from -36 to 36
- tissue_mask: int32 [256, 32, 4], P('slab', 'tile'), may hold values 0 or 1
Outputs:
- flow_field: float32 [2, 256, 32, 4], P(None, 'slab', 'tile')
- mesh_shift: float32 [2, 256, 32, 4], P(None, 'slab', 'tile')
The draws below stay inside these ranges and needn't reach their ends.
All inputs are finite; a program needn't handle non-finite values. No bound on the sum of `tissue_mask` on one device may be relied on, other than what follows from the above.
Results may differ from the reference program's by a relative error of at most 0.0003.
Values sent between devices are 32-bit elements; how exact they have to be, the bound alone decides.
A program may use at most 128 MiB of HBM per device.

```python
import jax
import jax.numpy as jnp
from jax import lax

COLS = 256
PATCH = 128
STRIDE = 64
TEMP = 256
STEPS = 4
SECTIONS = 256
ROWS = 2048
RIM = 32
NODE_ROWS = 32
NODE_COLS = 4


def draw_images(key, part):
    key = jax.random.fold_in(key, 7)
    keys = jax.random.split(key, 5)
    margin = 8
    raw = jax.random.truncated_normal(keys[0], -4.0, 4.0, (ROWS + 2 * margin + 2, COLS + 2 * margin + 2), jnp.float32)
    texture = jnp.zeros((ROWS + 2 * margin, COLS + 2 * margin), jnp.float32)
    for down in range(3):
        for across in range(3):
            texture = texture + raw[down:down + ROWS + 2 * margin, across:across + COLS + 2 * margin]
    texture = texture / 3.0
    cell_rows = ROWS // STRIDE
    cell_cols = COLS // STRIDE
    shift_rows = jax.random.randint(keys[1], (SECTIONS, cell_rows, cell_cols), -4, 5)
    shift_cols = jax.random.randint(keys[2], (SECTIONS, cell_rows, cell_cols), -4, 5)
    contrast = jax.random.uniform(keys[3], (SECTIONS,), jnp.float32, 0.4, 1.2)
    noise = 0.7 * jax.random.truncated_normal(keys[4], -4.0, 4.0, (SECTIONS, ROWS, COLS), jnp.float32)
    row_index = jnp.arange(ROWS)
    col_index = jnp.arange(COLS)

    def warped(index):
        moved_rows = shift_rows[index][row_index // STRIDE][:, col_index // STRIDE]
        moved_cols = shift_cols[index][row_index // STRIDE][:, col_index // STRIDE]
        return texture[row_index[:, None] + margin + moved_rows, col_index[None, :] + margin + moved_cols]
    moved = lax.map(warped, jnp.arange(SECTIONS))
    return contrast[:, None, None] * moved + noise


def set_ends(values, own_key, low, top_value):
    dims = values.shape
    spot = [jax.random.randint(jax.random.fold_in(own_key, axis), (), 0, dims[axis]) for axis in range(len(dims))]
    values = values.at[tuple(spot)].set(low)
    longest = dims.index(max(dims))
    spot[longest] = (spot[longest] + 1) % dims[longest]
    return values.at[tuple(spot)].set(top_value)


def setup_inputs(seed: int = 0) -> dict:
    arg_keys = jax.random.split(jax.random.key(seed), 3)
    images = draw_images(jax.random.fold_in(arg_keys[2], 71), 0)
    tissue_mask = set_ends((jax.random.randint(arg_keys[1], (SECTIONS, NODE_ROWS, NODE_COLS), 0, 4) < 3).astype(jnp.int32), jax.random.fold_in(arg_keys[1], 1), 0, 1)
    return {"images": images, "tissue_mask": tissue_mask}


inter_stiff = 1.0
plane_stiff = 0.25
step_size = 0.5
norm_eps = 1e-06

def lag_table(length):
    index = jnp.arange(length)
    return jnp.where(index < length // 2, index, index - length).astype(jnp.float32)

def patches_of(section):
    row_start = jnp.arange(NODE_ROWS) * STRIDE
    col_start = jnp.arange(NODE_COLS) * STRIDE
    rows = row_start[:, None] + jnp.arange(PATCH)[None, :]
    cols = col_start[:, None] + jnp.arange(PATCH)[None, :]
    return section[rows[:, None, :, None], cols[None, :, None, :]]

def soft_flow(earlier, later):
    spec_early = jnp.fft.fft2(earlier)
    spec_late = jnp.fft.fft2(later)
    corr = jnp.real(jnp.fft.ifft2(jnp.conj(spec_early) * spec_late))
    scores = corr / TEMP
    top = lax.optimization_barrier(jnp.max(scores, axis=(-2, -1), keepdims=True))
    weights = jnp.exp(scores - top)
    total = lax.optimization_barrier(jnp.sum(weights, axis=(-2, -1)))
    lags = lag_table(PATCH)
    flow_rows = lax.optimization_barrier(jnp.sum(weights * lags[:, None], axis=(-2, -1))) / total
    flow_cols = lax.optimization_barrier(jnp.sum(weights * lags[None, :], axis=(-2, -1))) / total
    return jnp.stack([flow_rows, flow_cols])

def forces(mesh, flow, spring):
    before = jnp.pad(mesh, ((0, 0), (1, 0), (0, 0), (0, 0)))[:, :-1]
    stretch = spring * (mesh - before - flow)
    stretch_next = jnp.pad(stretch, ((0, 0), (0, 1), (0, 0), (0, 0)))[:, 1:]
    framed = jnp.pad(mesh, ((0, 0), (0, 0), (1, 1), (1, 1)))
    beside_all = framed[:, :, :-2, 1:-1] + framed[:, :, 2:, 1:-1] + framed[:, :, 1:-1, :-2] + framed[:, :, 1:-1, 2:]
    return inter_stiff * (stretch_next - stretch) + plane_stiff * (beside_all - 4.0 * mesh)

def reference(images, tissue_mask):
    padded = jnp.pad(images, ((0, 0), (RIM, RIM), (RIM, RIM)))

    def pair_flow(index):
        earlier = patches_of(lax.dynamic_index_in_dim(padded, index - 1, 0, keepdims=False))
        later = patches_of(lax.dynamic_index_in_dim(padded, index, 0, keepdims=False))
        return soft_flow(earlier, later)
    rest = lax.map(pair_flow, jnp.arange(1, SECTIONS).astype(jnp.int32))
    first = jnp.zeros((1, 2, NODE_ROWS, NODE_COLS), jnp.float32)
    flow_field = jnp.transpose(jnp.concatenate([first, rest], axis=0), (1, 0, 2, 3))
    live = (jnp.arange(SECTIONS) > 0).astype(jnp.float32)
    spring = tissue_mask.astype(jnp.float32) * live[:, None, None]
    mesh = jnp.zeros((2, SECTIONS, NODE_ROWS, NODE_COLS), jnp.float32)
    for step in range(STEPS):
        force = forces(mesh, flow_field, spring)
        rms = jnp.sqrt(jnp.mean(force * force) + norm_eps)
        mesh = mesh + step_size * force / rms
    return (flow_field, mesh)
```

```python
import functools

import jax
import jax.numpy as jnp
import ml_dtypes
import numpy as np
from jax import lax
from jax.experimental import pallas as pl
from jax.experimental.pallas import tpu as pltpu
from jax.sharding import PartitionSpec as P

MESH = pl.DeviceIdType.MESH
PATCH = 128
STRIDE = 64
HALF = 64
RIM = 32
TEMP = 256
STEPS = 4
COLS = 256
NODES = 4
SEC = 4
ROWS = 256
WIDE = ROWS + 2 * RIM
LANES = 128

inter_stiff = 1.0
plane_stiff = 0.25
step_size = 0.5
norm_eps = 1e-06

f32 = jnp.float32
bf16 = jnp.bfloat16


def pieces(table):
    high = table.astype(np.float32).astype(ml_dtypes.bfloat16)
    low = (table - high.astype(np.float64)).astype(np.float32).astype(ml_dtypes.bfloat16)
    return high, low


def tables():
    k = np.arange(HALF)[:, None]
    x = np.arange(PATCH)[None, :]
    angle = 2.0 * np.pi * ((k * x) % PATCH) / PATCH
    cosine, sine = np.cos(angle), np.sin(angle)
    alternate = np.where(np.arange(PATCH) % 2 == 0, 1.0, -1.0)
    columns = np.zeros((COLS, 2, NODES, HALF))
    sine_slots = sine.copy()
    sine_slots[0] = alternate
    for j in range(NODES):
        for y in range(PATCH):
            col = j * STRIDE - RIM + y
            if 0 <= col < COLS:
                columns[col, 0, j] = cosine[:, y]
                columns[col, 1, j] = sine_slots[:, y]
    columns = columns.reshape(COLS, 2 * NODES * HALF)
    zero = np.zeros(PATCH)
    rows = np.zeros((4, HALF, 2, PATCH))
    rows[0, :, 0], rows[0, :, 1] = cosine, -sine
    rows[1, :, 0], rows[1, :, 1] = sine, cosine
    rows[2, :, 0], rows[2, :, 1] = cosine, sine
    rows[3, :, 0], rows[3, :, 1] = sine, -cosine
    rows[0, 0] = np.stack([zero + 1.0, zero])
    rows[1, 0] = np.stack([zero, zero + 1.0])
    rows[2, 0] = np.stack([alternate, zero])
    rows[3, 0] = np.stack([zero, alternate])
    back = np.zeros((2, PATCH, 4, HALF))
    for part, (c_part, s_part) in enumerate(((cosine, -sine), (sine, cosine), (cosine, sine), (sine, -cosine))):
        back[0, :, part] = c_part.T
        back[1, :, part] = s_part.T
    back[:, :, :, 0] = 0.0
    back[0, :, 0, 0] = 1.0
    back[1, :, 1, 0] = 1.0
    back[0, :, 2, 0] = alternate
    back[1, :, 3, 0] = alternate
    rows = rows.reshape(4 * HALF, 2 * PATCH)
    back = back.reshape(2 * PATCH, 4 * HALF)
    unit = np.log2(np.e) / (PATCH * PATCH * TEMP)
    cos_out, sin_out = 2.0 * unit * cosine, 2.0 * unit * sine_slots
    cos_out[0] = 0.25 * unit
    sin_out[0] = 0.25 * unit * alternate
    final = np.zeros((2, 2, HALF, 2, PATCH))
    for j in range(2):
        final[0, j, :, j] = cos_out
        final[1, j, :, j] = sin_out
    final = final.reshape(4 * HALF, 2 * PATCH)
    return [piece for table in (columns, rows, back, final) for piece in pieces(table)]


def split(x):
    high = x.astype(bf16)
    low = (x - high.astype(f32)).astype(bf16)
    return high, low


def dot(a, b):
    return jnp.dot(a, b, preferred_element_type=f32)


def dot3(a, b):
    return dot(a[0], b[0]) + dot(a[0], b[1]) + dot(a[1], b[0])


def iota(shape, dim):
    return lax.broadcasted_iota(jnp.int32, shape, dim)


def kernel(
    slabs,
    tiles,
    x_count,
    images,
    mask,
    cols_h,
    cols_l,
    rows_h,
    rows_l,
    back_h,
    back_l,
    last_h,
    last_l,
    flow_out,
    mesh_out,
    buf,
    z_h,
    z_l,
    spec,
    tops,
    sums,
    outgo,
    income,
    part,
    heard,
    local_sem,
    img_send,
    img_recv,
    halo_send,
    halo_recv,
    sum_send,
    sum_recv,
):
    z_count = slabs // x_count
    p = lax.axis_index("slab")
    t = lax.axis_index("tile")
    p_next, p_back = lax.rem(p + 1, slabs), lax.rem(p + slabs - 1, slabs)
    t_next, t_back = lax.rem(t + 1, tiles), lax.rem(t + tiles - 1, tiles)
    px, pz = lax.rem(p, x_count), lax.div(p, x_count)
    around = [(a, b) for a in (p_back, p, p_next) for b in (t_back, t, t_next)]
    around = [(n, d) for n, d in enumerate(around) if n != 4]

    def others(phase):
        if phase == 0:
            return [(p, lax.rem(t + d, tiles)) for d in range(1, tiles)]
        if phase == 1:
            return [(pz * x_count + lax.rem(px + d, x_count), t) for d in range(1, x_count)]
        return [(lax.rem(pz + d, z_count) * x_count + px, t) for d in range(1, z_count)]

    partners = [d for _, d in around] + [d for phase in range(3) for d in others(phase)]

    own = pltpu.make_async_copy(images, buf.at[pl.ds(1, SEC), pl.ds(RIM, ROWS), :], local_sem)
    own.start()
    barrier = pltpu.get_barrier_semaphore()
    for device in partners:
        pl.semaphore_signal(barrier, inc=1, device_id=device, device_id_type=MESH)
    pl.semaphore_wait(barrier, len(partners))

    top_rim, bottom_rim, middle = pl.ds(0, RIM), pl.ds(RIM + ROWS, RIM), pl.ds(RIM, ROWS)
    first_rows, last_rows = pl.ds(0, RIM), pl.ds(ROWS - RIM, RIM)
    sections = pl.ds(1, SEC)
    moves = [
        (images.at[:, last_rows, :], buf.at[sections, top_rim, :], (p, t_next)),
        (images.at[:, first_rows, :], buf.at[sections, bottom_rim, :], (p, t_back)),
        (images.at[pl.ds(SEC - 1, 1)], buf.at[pl.ds(0, 1), middle, :], (p_next, t)),
        (images.at[pl.ds(SEC - 1, 1), last_rows, :], buf.at[pl.ds(0, 1), top_rim, :], (p_next, t_next)),
        (images.at[pl.ds(SEC - 1, 1), first_rows, :], buf.at[pl.ds(0, 1), bottom_rim, :], (p_next, t_back)),
    ]
    copies = [
        pltpu.make_async_remote_copy(
            src_ref=src,
            dst_ref=dst,
            send_sem=img_send.at[n],
            recv_sem=img_recv.at[n],
            device_id=device,
            device_id_type=MESH,
        )
        for n, (src, dst, device) in enumerate(moves)
    ]
    for copy in copies:
        copy.start()

    def transform_columns(s, start, count):
        x_h, x_l = split(buf[s, pl.ds(start, count), :])
        z = dot(x_h, cols_h[...]) + dot(x_l, cols_h[...]) + dot(x_h, cols_l[...])
        high, low = split(z)
        z_h[s, pl.ds(start, count), :] = high
        z_l[s, pl.ds(start, count), :] = low

    def transform_rims(s):
        @pl.when(t == 0)
        def _():
            buf[s, top_rim, :] = jnp.zeros((RIM, COLS), f32)

        @pl.when(t == tiles - 1)
        def _():
            buf[s, bottom_rim, :] = jnp.zeros((RIM, COLS), f32)

        transform_columns(s, 0, RIM)
        transform_columns(s, RIM + ROWS, RIM)

    own.wait()

    @pl.loop(1, SEC + 1)
    def _(s):
        transform_columns(s, RIM, ROWS)

    copies[0].wait()
    copies[1].wait()

    @pl.loop(1, SEC + 1)
    def _(s):
        transform_rims(s)

    slot = lax.rem(iota((HALF, COLS), 1), HALF)
    inner_rows = iota((HALF, COLS), 0) > 0
    edge = (slot == 0) & inner_rows
    corner = (iota((8, COLS), 0) == 0) & (lax.rem(iota((8, COLS), 1), HALF) == 0)
    lag = iota((PATCH, 1), 0)
    lag = jnp.where(lag < PATCH // 2, lag, lag - PATCH).astype(f32)

    def quarters(x):
        return [x[n * HALF : (n + 1) * HALF] for n in range(4)]

    def spectrum(s, i):
        rows = pl.ds(i * STRIDE, PATCH)
        stacked = [
            jnp.concatenate([z[s, rows, :COLS], z[s, rows, COLS:]], axis=0) for z in (z_h, z_l)
        ]
        full = dot3((rows_h[...], rows_l[...]), stacked)
        a, b, c, d = quarters(full)
        spec[s, i, 0:HALF] = jnp.where(edge, a + c, a)
        spec[s, i, HALF : 2 * HALF] = jnp.where(edge, b + d, b)
        spec[s, i, 2 * HALF : 3 * HALF] = jnp.where(edge, b - d, c)
        spec[s, i, 3 * HALF :] = jnp.where(edge, c - a, d)

    def patched(general, special):
        return jnp.concatenate([jnp.where(corner, special, general[:8]), general[8:]], axis=0)

    def pair(earlier, i):
        ap, aq, ar, at = quarters(spec[earlier, i])
        bp, bq, br, bt = quarters(spec[earlier + 1, i])
        xp = patched(ap * bp + aq * bq, 4.0 * ap[:8] * bp[:8])
        xq = patched(ap * bq - aq * bp, 4.0 * aq[:8] * bq[:8])
        xr = patched(ar * br + at * bt, 4.0 * ar[:8] * br[:8])
        xt = patched(ar * bt - at * br, 4.0 * at[:8] * bt[:8])
        cross = jnp.concatenate(
            [
                jnp.where(edge, xp - xt, xp),
                jnp.where(edge, xq + xr, xq),
                jnp.where(edge, xp + xt, xr),
                jnp.where(edge, xq - xr, xt),
            ],
            axis=0,
        )
        u = split(dot3((back_h[...], back_l[...]), split(cross)))
        for half in range(2):
            lanes = slice(half * LANES, (half + 1) * LANES)
            u_h, u_l = (jnp.concatenate([x[:PATCH, lanes], x[PATCH:, lanes]], axis=1) for x in u)
            scores = dot(u_h, last_h[...]) + dot(u_l, last_h[...]) + dot(u_h, last_l[...])
            top = jnp.max(scores, axis=0, keepdims=True)
            weights = jnp.exp2(scores - top)
            total = jnp.sum(weights, axis=0, keepdims=True)
            moment = jnp.sum(weights * lag, axis=0, keepdims=True)
            place = slice(half * COLS, (half + 1) * COLS)
            tops[i, pl.ds(earlier, 1), place] = top
            tops[i, pl.ds(earlier + SEC, 1), place] = top
            sums[i, pl.ds(earlier, 1), place] = total
            sums[i, pl.ds(earlier + SEC, 1), place] = moment

    @pl.loop(0, SEC + 1)
    def _(m):
        s = lax.rem(m + 1, SEC + 1)

        @pl.when(m == SEC)
        def _():
            for copy in copies[2:]:
                copy.wait()
            transform_columns(0, RIM, ROWS)
            transform_rims(0)

        for i in range(NODES):
            spectrum(s, i)

        @pl.when(m > 0)
        def _():
            for i in range(NODES):
                pair(lax.rem(m, SEC), i)

    lane8 = iota((8, LANES), 1)
    row8 = iota((8, LANES), 0)
    lag_cols = jnp.where(lane8 < PATCH // 2, lane8, lane8 - PATCH).astype(f32)
    tile = jnp.zeros((8, LANES), f32)
    for i in range(NODES):
        for j in range(NODES):
            lanes = slice(j * LANES, (j + 1) * LANES)
            top = tops[i, :, lanes]
            scaled = sums[i, :, lanes] * jnp.exp2(top - jnp.max(top, axis=1, keepdims=True))
            both = jnp.sum(scaled, axis=1, keepdims=True)
            across = jnp.sum(scaled * lag_cols, axis=1, keepdims=True)
            total = both[:SEC]
            node = i * NODES + j
            flow_rows = jnp.concatenate([both[SEC:] / total, jnp.zeros((SEC, 1), f32)], axis=0)
            flow_cols = jnp.concatenate([across[:SEC] / total, jnp.zeros((SEC, 1), f32)], axis=0)
            tile = jnp.where(lane8 == node, flow_rows, tile)
            tile = jnp.where(lane8 == HALF + node, flow_cols, tile)
    live = (row8 % SEC + p > 0).astype(f32)
    spring = jnp.zeros((SEC, LANES), f32)
    for i in range(NODES):
        here = jnp.concatenate([mask[s, i : i + 1, :] for s in range(SEC)], axis=0).astype(f32)
        here = jnp.concatenate([here, jnp.zeros((SEC, LANES - NODES), f32)], axis=1)
        spring = spring + (pltpu.roll(here, i * NODES, 1) if i else here)
    spring = jnp.concatenate([jnp.zeros((SEC, LANES), f32), spring], axis=0)
    spring = spring + pltpu.roll(spring, HALF, 1)
    tile = (tile + spring) * live

    def write(out, x, shift):
        for c in range(2):
            for i in range(NODES):
                offset = (c * HALF + shift + i * NODES) % LANES
                moved = pltpu.roll(x, LANES - offset, 1) if offset else x
                for s in range(SEC):
                    out[c, s, i : i + 1, :] = moved[s : s + 1, :NODES]

    for n in range(3):
        outgo[n] = pltpu.roll(tile, 16 * n, 1) if n else tile
    halo = []
    for n, device in around:
        copy = pltpu.make_async_remote_copy(
            src_ref=outgo.at[2 - n % 3],
            dst_ref=income.at[8 - n],
            send_sem=halo_send.at[n],
            recv_sem=halo_recv.at[8 - n],
            device_id=device,
            device_id_type=MESH,
        )
        copy.start()
        halo.append(copy)
    write(flow_out, tile, 0)
    for copy in halo:
        copy.wait()

    blocks = []
    t_low, t_high = (t > 0).astype(f32), (t < tiles - 1).astype(f32)
    p_low, p_high = (p > 0).astype(f32), (p < slabs - 1).astype(f32)
    for a, there in enumerate((p_low, 1.0, p_high)):
        centre = outgo[1] if a == 1 else income[3 * a + 1]
        blocks.append(there * (t_low * income[3 * a] + centre + t_high * income[3 * a + 2]))
    zeros4 = jnp.zeros((SEC, LANES), f32)
    flow = jnp.concatenate([b[:SEC] for b in blocks] + [zeros4], axis=0)
    spring = jnp.concatenate([b[SEC:] for b in blocks] + [zeros4], axis=0)
    wide = 4 * SEC
    lane = lax.rem(iota((wide, LANES), 1), HALF)
    node_row, node_col = lax.div(lane, NODES), lax.rem(lane, NODES)
    inside = (node_row < 3 * NODES) & ((node_row >= NODES) | (t > 0)) & ((node_row < 2 * NODES) | (t < tiles - 1))
    inside = inside.astype(f32)
    has_left, has_right = (node_col > 0).astype(f32), (node_col < NODES - 1).astype(f32)

    def differ(stretch):
        return inter_stiff * (pltpu.roll(stretch, wide - 1, 0) - stretch)

    def apply(v):
        stretch = spring * (v - pltpu.roll(v, 1, 0))
        beside = (
            pltpu.roll(v, NODES, 1)
            + pltpu.roll(v, LANES - NODES, 1)
            + has_left * pltpu.roll(v, 1, 1)
            + has_right * pltpu.roll(v, LANES - 1, 1)
        )
        return inside * (differ(stretch) + plane_stiff * (beside - 4.0 * v))

    powers = [differ(-spring * flow)]
    for _ in range(STEPS - 1):
        powers.append(apply(powers[-1]))
    mine = ((row8 >= SEC) & (lax.rem(lane8, HALF) >= 16) & (lax.rem(lane8, HALF) < 32)).astype(f32)
    cores = [v[:8] * mine for v in powers]
    grams = [(a, b) for a in range(STEPS) for b in range(a, STEPS)]
    packed = [jnp.sum(cores[a] * cores[b], axis=0, keepdims=True) for a, b in grams]
    value = jnp.concatenate(packed + [jnp.zeros((16 - len(grams), LANES), f32)], axis=0)

    base = 0
    for phase in range(3):
        devices = others(phase)
        if not devices:
            continue
        part[phase] = value
        sent = []
        for n, device in enumerate(devices):
            copy = pltpu.make_async_remote_copy(
                src_ref=part.at[phase],
                dst_ref=heard.at[base + n],
                send_sem=sum_send.at[base + n],
                recv_sem=sum_recv.at[base + n],
                device_id=device,
                device_id_type=MESH,
            )
            copy.start()
            sent.append(copy)
        for copy in sent:
            copy.wait()
        for n in range(len(devices)):
            value = value + heard[base + n]
        base += len(devices)

    totals = jnp.sum(value, axis=1, keepdims=True)
    gram = {}
    for n, (a, b) in enumerate(grams):
        gram[a, b] = gram[b, a] = totals[n : n + 1, :]
    count = 2 * SEC * NODES * NODES * slabs * tiles
    zero = jnp.zeros((1, 1), f32)
    force = [zero + 1.0, zero, zero, zero]
    moved = [zero] * STEPS
    for step in range(STEPS):
        square = zero
        for a in range(step + 1):
            square = square + force[a] * force[a] * gram[a, a]
            for b in range(a + 1, step + 1):
                square = square + 2.0 * force[a] * force[b] * gram[a, b]
        scale = step_size / jnp.sqrt(jnp.maximum(square, 0.0) / count + norm_eps)
        moved = [m + scale * f for m, f in zip(moved, force)]
        force = [f + (scale * force[n - 1] if n else 0.0) for n, f in enumerate(force)]
    mesh_shift = sum(m * v[SEC : 2 * SEC] for m, v in zip(moved, powers))
    write(mesh_out, mesh_shift, 16)


def local(slabs, tiles, images, tissue_mask):
    x_count = 4 if slabs % 4 == 0 else slabs
    group = tiles - 1 + x_count - 1 + slabs // x_count - 1
    vmem = pl.BlockSpec(memory_space=pltpu.VMEM)
    constants = tables()
    out = jax.ShapeDtypeStruct((2, SEC, NODES, NODES), f32)
    dma = pltpu.SemaphoreType.DMA
    return pl.pallas_call(
        functools.partial(kernel, slabs, tiles, x_count),
        out_shape=(out, out),
        in_specs=[pl.BlockSpec(memory_space=pl.ANY), vmem] + [vmem] * len(constants),
        out_specs=(vmem, vmem),
        scratch_shapes=[
            pltpu.VMEM((SEC + 1, WIDE, COLS), f32),
            pltpu.VMEM((SEC + 1, WIDE, 2 * COLS), bf16),
            pltpu.VMEM((SEC + 1, WIDE, 2 * COLS), bf16),
            pltpu.VMEM((SEC + 1, NODES, 4 * HALF, COLS), f32),
            pltpu.VMEM((NODES, 2 * SEC, NODES * LANES), f32),
            pltpu.VMEM((NODES, 2 * SEC, NODES * LANES), f32),
            pltpu.VMEM((3, 8, LANES), f32),
            pltpu.VMEM((9, 8, LANES), f32),
            pltpu.VMEM((3, 16, LANES), f32),
            pltpu.VMEM((group, 16, LANES), f32),
            dma,
            dma((5,)),
            dma((5,)),
            dma((9,)),
            dma((9,)),
            dma((group,)),
            dma((group,)),
        ],
        compiler_params=pltpu.CompilerParams(
            collective_id=0, has_side_effects=True, vmem_limit_bytes=48 * 1024 * 1024
        ),
    )(images, tissue_mask, *[jnp.asarray(c) for c in constants])


def solution(mesh):
    placed = (P("slab", "tile", None), P("slab", "tile", None))
    return jax.shard_map(
        functools.partial(local, mesh.shape["slab"], mesh.shape["tile"]),
        mesh=mesh,
        in_specs=placed,
        out_specs=(P(None, "slab", "tile", None), P(None, "slab", "tile", None)),
        check_vma=False,
    )
```

```python
import functools

import jax
import jax.numpy as jnp
import ml_dtypes
import numpy as np
from jax import lax
from jax.experimental import pallas as pl
from jax.experimental.pallas import tpu as pltpu
from jax.sharding import PartitionSpec as P

MESH = pl.DeviceIdType.MESH
PATCH = 128
STRIDE = 64
HALF = 64
RIM = 32
TEMP = 256
STEPS = 4
BLOCK = 16
X_COUNT = 4
COLS = 256
NODES = 4
SEC = 4
ROWS = 256
WIDE = ROWS + 2 * RIM
LANES = 128

inter_stiff = 1.0
plane_stiff = 0.25
step_size = 0.5
norm_eps = 1e-06

f32 = jnp.float32
bf16 = jnp.bfloat16


def pieces(table):
    high = table.astype(np.float32).astype(ml_dtypes.bfloat16)
    low = (table - high.astype(np.float64)).astype(np.float32).astype(ml_dtypes.bfloat16)
    return high, low


def tables():
    k = np.arange(HALF)[:, None]
    x = np.arange(PATCH)[None, :]
    angle = 2.0 * np.pi * ((k * x) % PATCH) / PATCH
    cosine, sine = np.cos(angle), np.sin(angle)
    alternate = np.where(np.arange(PATCH) % 2 == 0, 1.0, -1.0)
    columns = np.zeros((COLS, 2, NODES, HALF))
    sine_slots = sine.copy()
    sine_slots[0] = alternate
    for j in range(NODES):
        for y in range(PATCH):
            col = j * STRIDE - RIM + y
            if 0 <= col < COLS:
                columns[col, 0, j] = cosine[:, y]
                columns[col, 1, j] = sine_slots[:, y]
    zero = np.zeros(PATCH)
    rows = np.zeros((4, HALF, 2, PATCH))
    rows[0, :, 0], rows[0, :, 1] = cosine, -sine
    rows[1, :, 0], rows[1, :, 1] = sine, cosine
    rows[2, :, 0], rows[2, :, 1] = cosine, sine
    rows[3, :, 0], rows[3, :, 1] = sine, -cosine
    rows[0, 0] = np.stack([zero + 1.0, zero])
    rows[1, 0] = np.stack([zero, zero + 1.0])
    rows[2, 0] = np.stack([alternate, zero])
    rows[3, 0] = np.stack([zero, alternate])
    back = np.zeros((2, PATCH, 4, HALF))
    for part, (c_part, s_part) in enumerate(((cosine, -sine), (sine, cosine), (cosine, sine), (sine, -cosine))):
        back[0, :, part] = c_part.T
        back[1, :, part] = s_part.T
    back[:, :, :, 0] = 0.0
    back[0, :, 0, 0] = 1.0
    back[1, :, 1, 0] = 1.0
    back[0, :, 2, 0] = alternate
    back[1, :, 3, 0] = alternate
    rows = rows.reshape(4 * HALF, 2 * PATCH)
    back = back.reshape(2 * PATCH, 4 * HALF)
    unit = np.log2(np.e) / (PATCH * PATCH * TEMP)
    cos_out, sin_out = 2.0 * unit * cosine, 2.0 * unit * sine_slots
    cos_out[0] = 0.25 * unit
    sin_out[0] = 0.25 * unit * alternate
    final = np.zeros((2, 2, HALF, 2, PATCH))
    for j in range(2):
        final[0, j, :, j] = cos_out
        final[1, j, :, j] = sin_out
    final = final.reshape(4 * HALF, 2 * PATCH)
    columns = columns.reshape(COLS, 2, NODES * HALF)
    parts = [piece for table in (columns[:, 0], columns[:, 1], rows, back, final) for piece in pieces(table)]
    return np.stack(parts)


def split(x):
    high = x.astype(bf16)
    low = (x - high.astype(f32)).astype(bf16)
    return high, low


def dot(a, b):
    return jnp.dot(a, b, preferred_element_type=f32)


def dot3(a, b):
    return dot(a[0], b[0]) + dot(a[0], b[1]) + dot(a[1], b[0])


def iota(shape, dim):
    return lax.broadcasted_iota(jnp.int32, shape, dim)


def quarters(x):
    return [x[n * HALF : (n + 1) * HALF] for n in range(4)]


def kernel(
    slabs,
    tiles,
    images,
    mask_in,
    table_in,
    flow_out,
    mesh_out,
    buf,
    mask,
    table,
    z_h,
    z_l,
    spec,
    tops,
    sums,
    outbox,
    inbox,
    plane_sum,
    local_sem,
    img_send,
    img_recv,
    flow_send,
    flow_recv,
    sum_send,
    sum_recv,
):
    z_count = slabs // X_COUNT
    plane = X_COUNT * tiles
    p = lax.axis_index("slab")
    t = lax.axis_index("tile")
    p_next, p_back = lax.rem(p + 1, slabs), lax.rem(p + slabs - 1, slabs)
    t_next, t_back = lax.rem(t + 1, tiles), lax.rem(t + tiles - 1, tiles)
    px, pz = lax.rem(p, X_COUNT), lax.div(p, X_COUNT)
    z_next, z_back = lax.rem(pz + 1, z_count), lax.rem(pz + z_count - 1, z_count)
    at_low, at_high = px == 0, px == X_COUNT - 1

    def in_plane(n):
        x = lax.rem(px + lax.div(n, tiles), X_COUNT)
        return (pz * X_COUNT + x, lax.rem(t + lax.rem(n, tiles), tiles))

    def along_z(n):
        return (lax.rem(pz + n, z_count) * X_COUNT + px, t)

    def signal(device):
        pl.semaphore_signal(barrier, inc=1, device_id=device, device_id_type=MESH)

    own = pltpu.make_async_copy(images, buf.at[pl.ds(1, SEC), pl.ds(RIM, ROWS), :], local_sem.at[0])
    first_tables = pltpu.make_async_copy(table_in.at[pl.ds(0, 4)], table.at[pl.ds(0, 4)], local_sem.at[1])
    other_tables = pltpu.make_async_copy(table_in.at[pl.ds(4, 6)], table.at[pl.ds(4, 6)], local_sem.at[2])
    own_mask = pltpu.make_async_copy(mask_in, mask, local_sem.at[3])
    for copy in (own, first_tables, other_tables, own_mask):
        copy.start()

    barrier = pltpu.get_barrier_semaphore()

    @pl.loop(0, tiles)
    def _(n):
        signal((z_back * X_COUNT + X_COUNT - 1, n))
        signal((z_next * X_COUNT, n))

    @pl.loop(1, plane)
    def _(n):
        signal(in_plane(n))

    @pl.loop(1, z_count)
    def _(n):
        signal(along_z(n))

    def remote(src, dst, send_sem, recv_sem, device):
        return pltpu.make_async_remote_copy(
            src_ref=src,
            dst_ref=dst,
            send_sem=send_sem,
            recv_sem=recv_sem,
            device_id=device,
            device_id_type=MESH,
        )

    top_rim, bottom_rim, middle = pl.ds(0, RIM), pl.ds(RIM + ROWS, RIM), pl.ds(RIM, ROWS)
    first_rows, last_rows = pl.ds(0, RIM), pl.ds(ROWS - RIM, RIM)
    sections, last, below = pl.ds(1, SEC), pl.ds(SEC - 1, 1), pl.ds(0, 1)
    moves = [
        (images.at[last], buf.at[below, middle, :], (p_next, t)),
        (images.at[last, last_rows, :], buf.at[below, top_rim, :], (p_next, t_next)),
        (images.at[last, first_rows, :], buf.at[below, bottom_rim, :], (p_next, t_back)),
        (images.at[:, last_rows, :], buf.at[sections, top_rim, :], (p, t_next)),
        (images.at[:, first_rows, :], buf.at[sections, bottom_rim, :], (p, t_back)),
    ]
    copies = [remote(src, dst, img_send.at[n], img_recv.at[n], device) for n, (src, dst, device) in enumerate(moves)]

    def transform_columns(s, start, count):
        rows = pl.ds(start, count)
        x = split(buf[s, rows, :])
        for n in range(2):
            high, low = split(dot3(x, (table[2 * n], table[2 * n + 1])))
            z_h[s, n, rows, :] = high
            z_l[s, n, rows, :] = low

    def transform_rims(s):
        @pl.when(t == 0)
        def _():
            buf[s, top_rim, :] = jnp.zeros((RIM, COLS), f32)

        @pl.when(t == tiles - 1)
        def _():
            buf[s, bottom_rim, :] = jnp.zeros((RIM, COLS), f32)

        transform_columns(s, 0, RIM)
        transform_columns(s, RIM + ROWS, RIM)

    slot = lax.rem(iota((HALF, COLS), 1), HALF)
    edge = (slot == 0) & (iota((HALF, COLS), 0) > 0)
    corner = (iota((8, COLS), 0) == 0) & (lax.rem(iota((8, COLS), 1), HALF) == 0)
    lag = iota((PATCH, 1), 0)
    lag = jnp.where(lag < PATCH // 2, lag, lag - PATCH).astype(f32)

    def spectrum(s, i):
        rows = pl.ds(pl.multiple_of(i * STRIDE, STRIDE), PATCH)
        stacked = [jnp.concatenate([z[s, 0, rows, :], z[s, 1, rows, :]], axis=0) for z in (z_h, z_l)]
        a, b, c, d = quarters(dot3((table[4], table[5]), stacked))
        spec[s, i, 0:HALF] = jnp.where(edge, a + c, a)
        spec[s, i, HALF : 2 * HALF] = jnp.where(edge, b + d, b)
        spec[s, i, 2 * HALF : 3 * HALF] = jnp.where(edge, b - d, c)
        spec[s, i, 3 * HALF :] = jnp.where(edge, c - a, d)

    def patched(general, special):
        return jnp.concatenate([jnp.where(corner, special, general[:8]), general[8:]], axis=0)

    def pair(earlier, i):
        ap, aq, ar, at = quarters(spec[earlier, i])
        bp, bq, br, bt = quarters(spec[earlier + 1, i])
        xp = patched(ap * bp + aq * bq, 4.0 * ap[:8] * bp[:8])
        xq = patched(ap * bq - aq * bp, 4.0 * aq[:8] * bq[:8])
        xr = patched(ar * br + at * bt, 4.0 * ar[:8] * br[:8])
        xt = patched(ar * bt - at * br, 4.0 * at[:8] * bt[:8])
        cross = jnp.concatenate(
            [
                jnp.where(edge, xp - xt, xp),
                jnp.where(edge, xq + xr, xq),
                jnp.where(edge, xp + xt, xr),
                jnp.where(edge, xq - xr, xt),
            ],
            axis=0,
        )
        u = split(dot3((table[6], table[7]), split(cross)))
        for half in range(2):
            lanes = slice(half * LANES, (half + 1) * LANES)
            stacked = [jnp.concatenate([x[:PATCH, lanes], x[PATCH:, lanes]], axis=1) for x in u]
            scores = dot3(stacked, (table[8], table[9]))
            top = jnp.max(scores, axis=0, keepdims=True)
            weights = jnp.exp2(scores - top)
            total = jnp.sum(weights, axis=0, keepdims=True)
            moment = jnp.sum(weights * lag, axis=0, keepdims=True)
            place = slice(half * COLS, (half + 1) * COLS)
            tops[i, pl.ds(earlier, 1), place] = top
            tops[i, pl.ds(earlier + SEC, 1), place] = top
            sums[i, pl.ds(earlier, 1), place] = total
            sums[i, pl.ds(earlier + SEC, 1), place] = moment

    first_tables.wait()
    own.wait()

    @pl.loop(1, SEC + 1)
    def _(s):
        transform_columns(s, RIM, ROWS)

    pl.semaphore_wait(barrier, plane - 1 + z_count - 1 + plane * jnp.where(at_low | at_high, 1, 0))
    for copy in copies:
        copy.start()
    other_tables.wait()

    @pl.loop(0, 2 * SEC)
    def _(m):
        outer = lax.div(m, SEC)
        step = lax.rem(m, SEC)

        @pl.when(m == SEC)
        def _():
            for copy in copies[3:]:
                copy.wait_recv()

            @pl.loop(1, SEC + 1)
            def _(s):
                transform_rims(s)

        rows = (1 - outer, 2 + outer)
        for i in rows:
            spectrum(step + 1, i)

        @pl.when(step > 0)
        def _():
            for i in rows:
                pair(step, i)

    for copy in copies[:3]:
        copy.wait_recv()
    transform_columns(0, RIM, ROWS)
    transform_rims(0)
    for i in range(NODES):
        spectrum(0, i)
    for i in range(NODES):
        pair(0, i)

    lane8 = iota((8, LANES), 1)
    row8 = iota((8, LANES), 0)
    lag_cols = jnp.where(lane8 < PATCH // 2, lane8, lane8 - PATCH).astype(f32)
    along = jnp.zeros((8, LANES), f32)
    across = jnp.zeros((8, LANES), f32)
    for i in range(NODES):
        for j in range(NODES):
            lanes = slice(j * LANES, (j + 1) * LANES)
            top = tops[i, :, lanes]
            scaled = sums[i, :, lanes] * jnp.exp2(top - jnp.max(top, axis=1, keepdims=True))
            here = lane8 == i * NODES + j
            along = jnp.where(here, jnp.sum(scaled, axis=1, keepdims=True), along)
            across = jnp.where(here, jnp.sum(scaled * lag_cols, axis=1, keepdims=True), across)
    live = lax.rem(row8, SEC) + p > 0
    low_half = row8 < SEC
    numerator = jnp.where(low_half, pltpu.roll(along, SEC, 0), pltpu.roll(across, SEC, 0))
    denominator = jnp.where(low_half, along, pltpu.roll(along, SEC, 0))
    flows = jnp.where(live & (lane8 < BLOCK), numerator / denominator, 0.0)

    own_mask.wait()
    springs = jnp.zeros((8, LANES), f32)
    for i in range(NODES):
        here = jnp.concatenate([mask[s, i : i + 1, :] for s in range(SEC)], axis=0).astype(f32)
        here = jnp.concatenate([here, jnp.zeros((SEC, LANES - NODES), f32)], axis=1)
        here = jnp.concatenate([here, jnp.zeros((SEC, LANES), f32)], axis=0)
        springs = springs + (pltpu.roll(here, i * NODES, 1) if i else here)
    springs = jnp.where(live, springs, 0.0)

    def flat(x):
        return jnp.sum(pltpu.roll(x, 0, 1, stride=BLOCK, stride_axis=0), axis=0, keepdims=True)

    outbox[0:1, :] = flat(flows)
    outbox[1:2, :] = flat(springs)
    inbox[1 + px, t] = outbox[...]

    def to_plane(n):
        return remote(outbox, inbox.at[1 + px, t], flow_send.at[n], flow_recv.at[1 + px, t], in_plane(n))

    def to_next(n):
        return remote(outbox, inbox.at[0, t], flow_send.at[plane + n], flow_recv.at[0, t], (z_next * X_COUNT + lax.div(n, tiles), lax.rem(n, tiles)))

    def to_back(n):
        return remote(outbox, inbox.at[X_COUNT + 1, t], flow_send.at[plane + n], flow_recv.at[X_COUNT + 1, t], (z_back * X_COUNT + lax.div(n, tiles), lax.rem(n, tiles)))

    def from_source(q, n):
        return remote(outbox, inbox.at[q, n], flow_send.at[0], flow_recv.at[q, n], (p_next, t))

    def write(out, x):
        for i in range(NODES):
            moved = pltpu.roll(x, LANES - i * NODES, 1) if i else x
            for c in range(2):
                for s in range(SEC):
                    out[c, s, i : i + 1, :] = moved[c * SEC + s : c * SEC + s + 1, :NODES]


    @pl.when(at_high)
    def _():
        @pl.loop(0, plane)
        def _(n):
            to_next(n).start()

    @pl.when(at_low)
    def _():
        @pl.loop(0, plane)
        def _(n):
            to_back(n).start()

    @pl.loop(1, plane)
    def _(n):
        to_plane(n).start()

    write(flow_out, flows)


    @pl.loop(0, tiles)
    def _(n):
        from_source(0, n).wait_recv()
        from_source(X_COUNT + 1, n).wait_recv()

    @pl.loop(1, plane)
    def _(n):
        x = lax.rem(px + lax.div(n, tiles), X_COUNT)
        from_source(1 + x, lax.rem(t + lax.rem(n, tiles), tiles)).wait_recv()

    block = lax.div(lane8, BLOCK)

    def transpose_blocks(x):
        for bit in (1, 2, 4):
            row_bit, lane_bit = (row8 & bit) > 0, (block & bit) > 0
            up = pltpu.roll(pltpu.roll(x, 8 - bit, 0), BLOCK * bit, 1)
            down = pltpu.roll(pltpu.roll(x, bit, 0), LANES - BLOCK * bit, 1)
            x = jnp.where(row_bit == lane_bit, x, jnp.where(row_bit, down, up))
        return x

    flow_parts, spring_parts = [], []
    for q in range(X_COUNT + 2):
        there = 1.0
        if q == 0:
            there = (pz > 0).astype(f32)
        elif q == X_COUNT + 1:
            there = (pz < z_count - 1).astype(f32)
        flow_q, spring_q = inbox[q, :, 0, :], inbox[q, :, 1, :]
        if tiles < 8:
            pad = jnp.zeros((8 - tiles, LANES), f32)
            flow_q, spring_q = (jnp.concatenate([v, pad], axis=0) for v in (flow_q, spring_q))
        flow_parts.append(there * transpose_blocks(flow_q))
        spring_parts.append(there * transpose_blocks(spring_q)[:SEC])
    wide = (X_COUNT + 2) * SEC
    spring = jnp.concatenate(spring_parts, axis=0)
    flow = [jnp.concatenate([v[c * SEC : (c + 1) * SEC] for v in flow_parts], axis=0) for c in range(2)]
    lane = iota((wide, LANES), 1)
    node_col = lax.rem(lane, NODES)
    live_lanes = (lane < tiles * BLOCK).astype(f32)
    has_up, has_down = (lane >= NODES).astype(f32), (lane < LANES - NODES).astype(f32)
    has_left, has_right = (node_col > 0).astype(f32), (node_col < NODES - 1).astype(f32)

    def differ(stretch):
        return inter_stiff * (pltpu.roll(stretch, wide - 1, 0) - stretch)

    def apply(v):
        stretch = spring * (v - pltpu.roll(v, 1, 0))
        beside = (
            has_up * pltpu.roll(v, NODES, 1)
            + has_down * pltpu.roll(v, LANES - NODES, 1)
            + has_left * pltpu.roll(v, 1, 1)
            + has_right * pltpu.roll(v, LANES - 1, 1)
        )
        return live_lanes * (differ(stretch) + plane_stiff * (beside - 4.0 * v))

    powers = []
    for c in range(2):
        chain = [differ(-spring * flow[c])]
        for _ in range(STEPS - 1):
            chain.append(apply(chain[-1]))
        powers.append(chain)
    grams = [(a, b) for a in range(STEPS) for b in range(a, STEPS)]
    core = slice(SEC, SEC + X_COUNT * SEC)
    rows = [
        jnp.sum(powers[0][a][core] * powers[0][b][core] + powers[1][a][core] * powers[1][b][core], axis=0, keepdims=True)
        for a, b in grams
    ]
    totals = jnp.concatenate(rows + [jnp.zeros((16 - len(grams), LANES), f32)], axis=0)
    totals = jnp.sum(totals, axis=1, keepdims=True)
    diagonal = iota((16, LANES), 0) == iota((16, LANES), 1)
    plane_sum[0:1, :] = jnp.sum(jnp.where(diagonal, totals, 0.0), axis=0, keepdims=True)

    def to_z(n):
        return remote(plane_sum.at[pl.ds(0, 1)], plane_sum.at[pl.ds(n, 1)], sum_send.at[n], sum_recv.at[n], along_z(n))


    @pl.loop(1, z_count)
    def _(n):
        to_z(n).start()

    mine = []
    for a in range(STEPS):
        both = jnp.zeros((8, LANES), f32)
        for q in range(X_COUNT):
            part = slice(SEC + q * SEC, 2 * SEC + q * SEC)
            here = jnp.concatenate([powers[0][a][part], powers[1][a][part]], axis=0)
            both = jnp.where(px == q, here, both)
        mine.append(pltpu.roll(both, lax.rem(LANES - t * BLOCK, LANES), 1))

    for copy in copies:
        copy.wait_send()

    @pl.when(at_low | at_high)
    def _():
        @pl.loop(0, plane)
        def _(n):
            to_next(n).wait_send()

    @pl.loop(1, plane)
    def _(n):
        to_plane(n).wait_send()

    @pl.loop(1, z_count)
    def _(n):
        to_z(n).wait_recv()

    totals = jnp.sum(plane_sum[0:z_count], axis=0, keepdims=True)
    gram = {}
    for n, (a, b) in enumerate(grams):
        gram[a, b] = gram[b, a] = totals[:, n : n + 1]
    count = 2 * SEC * NODES * NODES * slabs * tiles
    zero = jnp.zeros((1, 1), f32)
    force = [zero + 1.0, zero, zero, zero]
    moved = [zero] * STEPS
    for step in range(STEPS):
        square = zero
        for a in range(step + 1):
            square = square + force[a] * force[a] * gram[a, a]
            for b in range(a + 1, step + 1):
                square = square + 2.0 * force[a] * force[b] * gram[a, b]
        scale = step_size / jnp.sqrt(jnp.maximum(square, 0.0) / count + norm_eps)
        moved = [m + scale * f for m, f in zip(moved, force)]
        force = [f + (scale * force[n - 1] if n else 0.0) for n, f in enumerate(force)]
    write(mesh_out, sum(m * v for m, v in zip(moved, mine)))

    @pl.loop(1, z_count)
    def _(n):
        to_z(n).wait_send()


def local(slabs, tiles, images, tissue_mask):
    z_count = max(slabs // X_COUNT, 1)
    plane = X_COUNT * tiles
    vmem = pl.BlockSpec(memory_space=pltpu.VMEM)
    hbm = pl.BlockSpec(memory_space=pltpu.HBM)
    constants = jnp.asarray(tables())
    out = jax.ShapeDtypeStruct((2, SEC, NODES, NODES), f32)
    dma = pltpu.SemaphoreType.DMA
    return pl.pallas_call(
        functools.partial(kernel, slabs, tiles),
        out_shape=(out, out),
        in_specs=[hbm, hbm, hbm],
        out_specs=(vmem, vmem),
        scratch_shapes=[
            pltpu.VMEM((SEC + 1, WIDE, COLS), f32),
            pltpu.VMEM((SEC, NODES, NODES), jnp.int32),
            pltpu.VMEM(constants.shape, bf16),
            pltpu.VMEM((SEC + 1, 2, WIDE, COLS), bf16),
            pltpu.VMEM((SEC + 1, 2, WIDE, COLS), bf16),
            pltpu.VMEM((SEC + 1, NODES, 4 * HALF, COLS), f32),
            pltpu.VMEM((NODES, 2 * SEC, NODES * LANES), f32),
            pltpu.VMEM((NODES, 2 * SEC, NODES * LANES), f32),
            pltpu.VMEM((2, LANES), f32),
            pltpu.VMEM((X_COUNT + 2, tiles, 2, LANES), f32),
            pltpu.VMEM((max(z_count, 8), LANES), f32),
            dma((4,)),
            dma((5,)),
            dma((5,)),
            dma((2 * plane,)),
            dma((X_COUNT + 2, tiles)),
            dma((z_count,)),
            dma((z_count,)),
        ],
        compiler_params=pltpu.CompilerParams(
            collective_id=0, has_side_effects=True, vmem_limit_bytes=64 * 1024 * 1024 - 65536
        ),
    )(images, tissue_mask, constants)


def solution(mesh):
    placed = (P("slab", "tile", None), P("slab", "tile", None))
    return jax.shard_map(
        functools.partial(local, mesh.shape["slab"], mesh.shape["tile"]),
        mesh=mesh,
        in_specs=placed,
        out_specs=(P(None, "slab", "tile", None), P(None, "slab", "tile", None)),
        check_vma=False,
    )
```

```python
import functools

import jax
import jax.numpy as jnp
import ml_dtypes
import numpy as np
from jax import lax
from jax.experimental import pallas as pl
from jax.experimental.pallas import tpu as pltpu
from jax.sharding import PartitionSpec as P

MESH = pl.DeviceIdType.MESH
PATCH = 128
STRIDE = 64
HALF = 64
RIM = 32
TEMP = 256
STEPS = 4
BLOCK = 16
SPLIT = 160
X_COUNT = 4
COLS = 256
NODES = 4
SEC = 4
ROWS = 256
WIDE = ROWS + 2 * RIM
LANES = 128

inter_stiff = 1.0
plane_stiff = 0.25
step_size = 0.5
norm_eps = 1e-06

f32 = jnp.float32
bf16 = jnp.bfloat16


def pieces(table):
    high = table.astype(np.float32).astype(ml_dtypes.bfloat16)
    low = (table - high.astype(np.float64)).astype(np.float32).astype(ml_dtypes.bfloat16)
    return high, low


def tables():
    k = np.arange(HALF)[:, None]
    x = np.arange(PATCH)[None, :]
    angle = 2.0 * np.pi * ((k * x) % PATCH) / PATCH
    cosine, sine = np.cos(angle), np.sin(angle)
    alternate = np.where(np.arange(PATCH) % 2 == 0, 1.0, -1.0)
    sine[0] = np.where(np.arange(PATCH) % 2 == 0, 1.0, -1.0)
    forward = np.concatenate([cosine, sine], axis=0)
    columns = np.zeros((2, COLS, NODES, HALF))
    for j in range(NODES):
        for y in range(PATCH):
            col = j * STRIDE - RIM + y
            if 0 <= col < COLS:
                columns[0, col, j] = cosine[:, y]
                columns[1, col, j] = sine[:, y]
    columns = columns.reshape(2, COLS, NODES * HALF)
    unit = 2.0 * np.log2(np.e) / (PATCH * PATCH * TEMP)
    final = np.zeros((2, 2, HALF, 2, PATCH))
    for j in range(2):
        final[0, j, :, j] = unit * cosine
        final[1, j, :, j] = unit * sine
    final = final.reshape(4 * HALF, 2 * PATCH)

    def stacked(table):
        high, low = pieces(table)
        return np.block([[high, high], [low, np.zeros_like(low)]])

    return np.stack(
        [stacked(forward), *pieces(columns[0]), *pieces(columns[1]), stacked(forward.T), *pieces(final)]
    )


def split(x):
    high = x.astype(bf16)
    low = (x - high.astype(f32)).astype(bf16)
    return high, low


def dot(a, b):
    return jnp.dot(a, b, preferred_element_type=f32)


def dot3(a, b):
    count = a.shape[0] // 2
    both = dot(a, b[0])
    return both[:count] + both[count:] + dot(a[:count], b[1])


def iota(shape, dim):
    return lax.broadcasted_iota(jnp.int32, shape, dim)


def quarters(x):
    return [x[n * HALF : (n + 1) * HALF] for n in range(4)]


def kernel(
    slabs,
    tiles,
    images,
    mask_in,
    table_in,
    flow_out,
    mesh_out,
    buf,
    mask,
    table,
    x_h,
    x_l,
    y,
    spec,
    first_spec,
    tops,
    sums,
    outbox,
    inbox,
    plane_sum,
    local_sem,
    img_send,
    img_recv,
    flow_send,
    flow_recv,
    sum_send,
    sum_recv,
):
    z_count = max(slabs // X_COUNT, 1)
    plane = X_COUNT * tiles
    p = lax.axis_index("slab")
    t = lax.axis_index("tile")
    p_next, p_back = lax.rem(p + 1, slabs), lax.rem(p + slabs - 1, slabs)
    t_next, t_back = lax.rem(t + 1, tiles), lax.rem(t + tiles - 1, tiles)
    px, pz = lax.rem(p, X_COUNT), lax.div(p, X_COUNT)
    z_next, z_back = lax.rem(pz + 1, z_count), lax.rem(pz + z_count - 1, z_count)
    at_low, at_high = px == 0, px == X_COUNT - 1

    x_ring = [lax.rem(px + a, X_COUNT) for a in range(X_COUNT)]
    t_ring = [lax.rem(t + b, tiles) for b in range(tiles)]
    z_ring = [lax.rem(pz + a, z_count) for a in range(z_count)]

    def hops(step, size):
        return min(step, size - step)

    steps = [(a, b) for a in range(X_COUNT) for b in range(tiles) if a or b]
    steps.sort(key=lambda ab: -hops(ab[0], X_COUNT) - hops(ab[1], tiles) / 2)
    plane_mates = [(pz * X_COUNT + x_ring[a], t_ring[b]) for a, b in steps]
    z_mates = [(z_ring[n] * X_COUNT + px, t) for n in sorted(range(1, z_count), key=lambda n: -hops(n, z_count))]

    def signal(device):
        pl.semaphore_signal(barrier, inc=1, device_id=device, device_id_type=MESH)

    own = pltpu.make_async_copy(images, buf.at[pl.ds(1, SEC), pl.ds(RIM, ROWS), :], local_sem.at[0])
    first_tables = pltpu.make_async_copy(table_in.at[pl.ds(0, 1)], table.at[pl.ds(0, 1)], local_sem.at[1])
    other_tables = pltpu.make_async_copy(table_in.at[pl.ds(1, 7)], table.at[pl.ds(1, 7)], local_sem.at[2])
    own_mask = pltpu.make_async_copy(mask_in, mask, local_sem.at[3])
    for copy in (own, first_tables, other_tables, own_mask):
        copy.start()

    barrier = pltpu.get_barrier_semaphore()

    for device in z_mates:
        signal(device)
    for n in range(tiles):
        signal((z_back * X_COUNT + X_COUNT - 1, n))
        signal((z_next * X_COUNT, n))
    for device in plane_mates:
        signal(device)

    def remote(src, dst, send_sem, recv_sem, device):
        return pltpu.make_async_remote_copy(
            src_ref=src,
            dst_ref=dst,
            send_sem=send_sem,
            recv_sem=recv_sem,
            device_id=device,
            device_id_type=MESH,
        )

    top_rim, bottom_rim = pl.ds(0, RIM), pl.ds(RIM + ROWS, RIM)
    first_rows, last_rows = pl.ds(0, RIM), pl.ds(ROWS - RIM, RIM)
    sections, last, below = pl.ds(1, SEC), pl.ds(SEC - 1, 1), pl.ds(0, 1)
    moves = [
        (images.at[last, pl.ds(0, SPLIT), :], buf.at[below, pl.ds(RIM, SPLIT), :], (p_next, t)),
        (images.at[last, last_rows, :], buf.at[below, top_rim, :], (p_next, t_next)),
        (images.at[last, pl.ds(SPLIT, ROWS - SPLIT), :], buf.at[below, pl.ds(RIM + SPLIT, ROWS - SPLIT), :], (p_next, t)),
        (images.at[last, first_rows, :], buf.at[below, bottom_rim, :], (p_next, t_back)),
        (images.at[:, last_rows, :], buf.at[sections, top_rim, :], (p, t_next)),
        (images.at[:, first_rows, :], buf.at[sections, bottom_rim, :], (p, t_back)),
    ]
    copies = [remote(src, dst, img_send.at[n], img_recv.at[n], device) for n, (src, dst, device) in enumerate(moves)]

    def prepare(s, start, count):
        rows = pl.ds(start, count)
        x_h[s, rows, :], x_l[s, rows, :] = split(buf[s, rows, :])

    def prepare_top(s):
        @pl.when(t == 0)
        def _():
            buf[s, top_rim, :] = jnp.zeros((RIM, COLS), f32)

        prepare(s, 0, RIM)

    def prepare_bottom(s):
        @pl.when(t == tiles - 1)
        def _():
            buf[s, bottom_rim, :] = jnp.zeros((RIM, COLS), f32)

        prepare(s, RIM + ROWS, RIM)

    row_zero = iota((8, COLS), 0) == 0
    lane_zero = lax.rem(iota((8, COLS), 1), HALF) == 0
    corner = row_zero & lane_zero
    lag = iota((PATCH, 1), 0)
    lag = jnp.where(lag < PATCH // 2, lag, lag - PATCH).astype(f32)

    def merged(general, at_lane, at_row):
        lanes = jnp.concatenate([lane_zero] * (HALF // 8), axis=0)
        out = jnp.where(lanes, at_lane, general)
        return jnp.concatenate([jnp.where(row_zero, at_row[:8], out[:8]), out[8:]], axis=0)

    def transform_rows(s, i, place, n):
        rows = pl.ds(pl.multiple_of(i * STRIDE, STRIDE), PATCH)
        window = jnp.concatenate([x_h[s, rows, :], x_l[s, rows, :]], axis=0)
        both = dot(table[0], window)
        high, low = split(both[:PATCH] + both[PATCH:])
        y[place, n * PATCH : (n + 1) * PATCH] = high
        y[place, (2 + n) * PATCH : (3 + n) * PATCH] = low

    def spectra(place):
        rows = y[place]
        c = dot3(rows, (table[1], table[2]))
        d = dot3(rows, (table[3], table[4]))
        found = []
        for n in range(2):
            cc, sc = c[2 * n * HALF : (2 * n + 1) * HALF], c[(2 * n + 1) * HALF : (2 * n + 2) * HALF]
            cs, ss = d[2 * n * HALF : (2 * n + 1) * HALF], d[(2 * n + 1) * HALF : (2 * n + 2) * HALF]
            found.append(
                [
                    merged(cc - ss, cc, cc),
                    merged(cs + sc, sc, cs),
                    merged(cc + ss, cs, sc),
                    merged(sc - cs, ss, ss),
                ]
            )
        return found

    def keep(ref, index, parts):
        for n, part in enumerate(parts):
            ref[index, n * HALF : (n + 1) * HALF] = part

    def patched(general, special):
        return jnp.concatenate([jnp.where(corner, special, general[:8]), general[8:]], axis=0)

    def correlate(first, second):
        ap, aq, ar, at = quarters(first)
        bp, bq, br, bt = quarters(second)
        xp = patched(ap * bp + aq * bq, 0.5 * ap[:8] * bp[:8])
        xq = patched(ap * bq - aq * bp, 0.5 * aq[:8] * bq[:8])
        xr = patched(ar * br + at * bt, 0.5 * ar[:8] * br[:8])
        xt = patched(ar * bt - at * br, 0.5 * at[:8] * bt[:8])
        cosines = split(jnp.concatenate([merged(xp + xr, xp, xp), merged(xq + xt, xq, xr)], axis=0))
        sines = split(jnp.concatenate([merged(xq - xt, xr, xq), merged(xr - xp, xt, xt)], axis=0))
        parts = []
        for v in (cosines, sines):
            both = dot(table[5], jnp.concatenate(v, axis=0))
            parts.append(split(both[:PATCH] + both[PATCH:]))
        (c_h, c_l), (s_h, s_l) = parts
        lanes = [slice(n * LANES, (n + 1) * LANES) for n in range(2)]
        high = [jnp.concatenate([c_h[:, k], s_h[:, k]], axis=1) for k in lanes]
        low = [jnp.concatenate([c_l[:, k], s_l[:, k]], axis=1) for k in lanes]
        return high, low

    def pairs(earlier, rows, firsts, seconds):
        high, low = [], []
        for first, second in zip(firsts, seconds):
            more_high, more_low = correlate(first, second)
            high += more_high
            low += more_low
        both = dot3(jnp.concatenate(high + low, axis=0), (table[6], table[7]))
        for n in range(2 * len(rows)):
            i, half = rows[n // 2], n % 2
            scores = both[n * PATCH : (n + 1) * PATCH]
            top = jnp.max(scores, axis=0, keepdims=True)
            weights = jnp.exp2(scores - top)
            total = jnp.sum(weights, axis=0, keepdims=True)
            moment = jnp.sum(weights * lag, axis=0, keepdims=True)
            place = slice(half * COLS, (half + 1) * COLS)
            tops[i, pl.ds(earlier, 1), place] = top
            tops[i, pl.ds(earlier + SEC, 1), place] = top
            sums[i, pl.ds(earlier, 1), place] = total
            sums[i, pl.ds(earlier + SEC, 1), place] = moment

    def begin():
        pl.semaphore_wait(barrier, plane - 1 + z_count - 1 + plane * jnp.where(at_low | at_high, 1, 0))
        for copy in copies:
            copy.start()

    own.wait()
    for s in range(1, SEC + 1):
        prepare(s, RIM, ROWS)
    first_tables.wait()
    for s in range(1, SEC + 1):
        for n in range(2):
            transform_rows(s, 1 + n, s, n)
    begin()
    other_tables.wait()

    @pl.loop(0, 2)
    def _(outer):
        rows = (1 - outer, 2 + outer)

        @pl.when(outer == 1)
        def _():
            for copy in copies[4:]:
                copy.wait_recv()
            for s in range(1, SEC + 1):
                prepare_top(s)
                prepare_bottom(s)
            for s in range(1, SEC + 1):
                for n in range(2):
                    transform_rows(s, 3 * n, s, n)

        for s in range(1, SEC + 1):
            for n, parts in enumerate(spectra(s)):
                if s == 1:
                    keep(first_spec, rows[n], parts)
                keep(spec, (s - 1) * 2 + n, parts)
            if s > 1:
                pairs(s - 1, rows, [spec[(s - 2) * 2 + n] for n in range(2)], [spec[(s - 1) * 2 + n] for n in range(2)])

    for n in range(2):
        for copy in copies[2 * n : 2 * n + 2]:
            copy.wait_recv()
        if n == 0:
            prepare_top(0)
            prepare(0, RIM, SPLIT)
        else:
            prepare(0, RIM + SPLIT, ROWS - SPLIT)
            prepare_bottom(0)
        rows = (2 * n, 2 * n + 1)
        for k in range(2):
            transform_rows(0, rows[k], n, k)
        for k, parts in enumerate(spectra(n)):
            keep(spec, rows[k], parts)
        pairs(0, rows, [spec[i] for i in rows], [first_spec[i] for i in rows])

    lane8 = iota((8, LANES), 1)
    row8 = iota((8, LANES), 0)
    lag_cols = jnp.where(lane8 < PATCH // 2, lane8, lane8 - PATCH).astype(f32)
    along = jnp.zeros((8, LANES), f32)
    across = jnp.zeros((8, LANES), f32)
    for i in range(NODES):
        for j in range(NODES):
            lanes = slice(j * LANES, (j + 1) * LANES)
            top = tops[i, :, lanes]
            scaled = sums[i, :, lanes] * jnp.exp2(top - jnp.max(top, axis=1, keepdims=True))
            here = lane8 == i * NODES + j
            along = jnp.where(here, jnp.sum(scaled, axis=1, keepdims=True), along)
            across = jnp.where(here, jnp.sum(scaled * lag_cols, axis=1, keepdims=True), across)
    live = lax.rem(row8, SEC) + p > 0
    low_half = row8 < SEC
    numerator = jnp.where(low_half, pltpu.roll(along, SEC, 0), pltpu.roll(across, SEC, 0))
    denominator = jnp.where(low_half, along, pltpu.roll(along, SEC, 0))
    flows = jnp.where(live & (lane8 < BLOCK), numerator / denominator, 0.0)

    own_mask.wait()
    springs = jnp.zeros((8, LANES), f32)
    for i in range(NODES):
        here = jnp.concatenate([mask[s, i : i + 1, :] for s in range(SEC)], axis=0).astype(f32)
        here = jnp.concatenate([here, jnp.zeros((SEC, LANES - NODES), f32)], axis=1)
        here = jnp.concatenate([here, jnp.zeros((SEC, LANES), f32)], axis=0)
        springs = springs + (pltpu.roll(here, i * NODES, 1) if i else here)
    springs = jnp.where(live, springs, 0.0)

    def flat(x):
        return jnp.sum(pltpu.roll(x, 0, 1, stride=BLOCK, stride_axis=0), axis=0, keepdims=True)

    outbox[0, 0:1, :] = flat(flows)
    outbox[0, 1:2, :] = flat(springs)
    inbox[(1 + px) * tiles + t] = outbox[0]

    def give(q, sem, device):
        return remote(outbox, inbox.at[pl.ds(q * tiles + t, 1)], flow_send.at[sem], flow_recv, device)

    def whole(ref, count, sem):
        slots = ref.at[pl.ds(0, count)]
        pltpu.make_async_copy(slots, slots, sem).wait()

    def write(out, x):
        for i in range(NODES):
            moved = pltpu.roll(x, LANES - i * NODES, 1) if i else x
            for c in range(2):
                for s in range(SEC):
                    out[c, s, i : i + 1, :] = moved[c * SEC + s : c * SEC + s + 1, :NODES]

    @pl.when(at_high)
    def _():
        for x in range(X_COUNT):
            for n in range(tiles):
                give(0, 1, (z_next * X_COUNT + x, n)).start()

    @pl.when(at_low)
    def _():
        for x in range(X_COUNT):
            for n in range(tiles):
                give(X_COUNT + 1, 1, (z_back * X_COUNT + x, n)).start()

    for device in plane_mates:
        give(1 + px, 0, device).start()

    write(flow_out, flows)

    whole(inbox, plane - 1 + 2 * tiles, flow_recv)

    block = lax.div(lane8, BLOCK)

    def transpose_blocks(x):
        for bit in (1, 2, 4):
            row_bit, lane_bit = (row8 & bit) > 0, (block & bit) > 0
            up = pltpu.roll(pltpu.roll(x, 8 - bit, 0), BLOCK * bit, 1)
            down = pltpu.roll(pltpu.roll(x, bit, 0), LANES - BLOCK * bit, 1)
            x = jnp.where(row_bit == lane_bit, x, jnp.where(row_bit, down, up))
        return x

    flow_parts, spring_parts = [], []
    for q in range(X_COUNT + 2):
        there = 1.0
        if q == 0:
            there = (pz > 0).astype(f32)
        elif q == X_COUNT + 1:
            there = (pz < z_count - 1).astype(f32)
        here = slice(q * tiles, (q + 1) * tiles)
        flow_q, spring_q = inbox[here, 0, :], inbox[here, 1, :]
        if tiles < 8:
            pad = jnp.zeros((8 - tiles, LANES), f32)
            flow_q, spring_q = (jnp.concatenate([v, pad], axis=0) for v in (flow_q, spring_q))
        flow_parts.append(there * transpose_blocks(flow_q))
        spring_parts.append(there * transpose_blocks(spring_q)[:SEC])
    wide = (X_COUNT + 2) * SEC
    spring = jnp.concatenate(spring_parts, axis=0)
    flow = [jnp.concatenate([v[c * SEC : (c + 1) * SEC] for v in flow_parts], axis=0) for c in range(2)]
    lane = iota((wide, LANES), 1)
    node_col = lax.rem(lane, NODES)
    live_lanes = (lane < tiles * BLOCK).astype(f32)
    has_up, has_down = (lane >= NODES).astype(f32), (lane < LANES - NODES).astype(f32)
    has_left, has_right = (node_col > 0).astype(f32), (node_col < NODES - 1).astype(f32)

    def differ(stretch):
        return inter_stiff * (pltpu.roll(stretch, wide - 1, 0) - stretch)

    def apply(v):
        stretch = spring * (v - pltpu.roll(v, 1, 0))
        beside = (
            has_up * pltpu.roll(v, NODES, 1)
            + has_down * pltpu.roll(v, LANES - NODES, 1)
            + has_left * pltpu.roll(v, 1, 1)
            + has_right * pltpu.roll(v, LANES - 1, 1)
        )
        return live_lanes * (differ(stretch) + plane_stiff * (beside - 4.0 * v))

    powers = []
    for c in range(2):
        chain = [differ(-spring * flow[c])]
        for _ in range(STEPS - 1):
            chain.append(apply(chain[-1]))
        powers.append(chain)
    grams = [(a, b) for a in range(STEPS) for b in range(a, STEPS)]
    core = slice(SEC, SEC + X_COUNT * SEC)
    rows = [
        jnp.sum(powers[0][a][core] * powers[0][b][core] + powers[1][a][core] * powers[1][b][core], axis=0, keepdims=True)
        for a, b in grams
    ]
    totals = jnp.concatenate(rows + [jnp.zeros((16 - len(grams), LANES), f32)], axis=0)
    totals = jnp.sum(totals, axis=1, keepdims=True)
    diagonal = iota((16, LANES), 0) == iota((16, LANES), 1)
    plane_sum[0] = jnp.sum(jnp.where(diagonal, totals, 0.0), axis=0, keepdims=True)

    def to_z(n):
        slot = pl.ds(n, 1)
        return remote(plane_sum.at[pl.ds(0, 1)], plane_sum.at[slot], sum_send, sum_recv, z_by_step[n])

    z_by_step = [(z_ring[n] * X_COUNT + px, t) for n in range(z_count)]
    for n in sorted(range(1, z_count), key=lambda n: -hops(n, z_count)):
        to_z(n).start()

    mine = []
    for a in range(STEPS):
        both = jnp.zeros((8, LANES), f32)
        for q in range(X_COUNT):
            part = slice(SEC + q * SEC, 2 * SEC + q * SEC)
            here = jnp.concatenate([powers[0][a][part], powers[1][a][part]], axis=0)
            both = jnp.where(px == q, here, both)
        mine.append(pltpu.roll(both, lax.rem(LANES - t * BLOCK, LANES), 1))

    for copy in copies:
        copy.wait_send()

    whole(inbox, plane - 1, flow_send.at[0])

    @pl.when(at_low | at_high)
    def _():
        whole(inbox, plane, flow_send.at[1])

    whole(plane_sum, z_count - 1, sum_recv)

    totals = jnp.sum(plane_sum[0:z_count, 0, :], axis=0, keepdims=True)
    gram = {}
    for n, (a, b) in enumerate(grams):
        gram[a, b] = gram[b, a] = totals[:, n : n + 1]
    count = 2 * SEC * NODES * NODES * slabs * tiles
    zero = jnp.zeros((1, 1), f32)
    force = [zero + 1.0, zero, zero, zero]
    moved = [zero] * STEPS
    for step in range(STEPS):
        square = zero
        for a in range(step + 1):
            square = square + force[a] * force[a] * gram[a, a]
            for b in range(a + 1, step + 1):
                square = square + 2.0 * force[a] * force[b] * gram[a, b]
        scale = step_size / jnp.sqrt(jnp.maximum(square, 0.0) / count + norm_eps)
        moved = [m + scale * f for m, f in zip(moved, force)]
        force = [f + (scale * force[n - 1] if n else 0.0) for n, f in enumerate(force)]
    write(mesh_out, sum(m * v for m, v in zip(moved, mine)))
    whole(plane_sum, z_count - 1, sum_send)


def local(slabs, tiles, images, tissue_mask):
    z_count = max(slabs // X_COUNT, 1)
    plane = X_COUNT * tiles
    vmem = pl.BlockSpec(memory_space=pltpu.VMEM)
    hbm = pl.BlockSpec(memory_space=pltpu.HBM)
    constants = jnp.asarray(tables())
    out = jax.ShapeDtypeStruct((2, SEC, NODES, NODES), f32)
    dma = pltpu.SemaphoreType.DMA
    return pl.pallas_call(
        functools.partial(kernel, slabs, tiles),
        out_shape=(out, out),
        in_specs=[hbm, hbm, hbm],
        out_specs=(vmem, vmem),
        scratch_shapes=[
            pltpu.VMEM((SEC + 1, WIDE, COLS), f32),
            pltpu.VMEM((SEC, NODES, NODES), jnp.int32),
            pltpu.VMEM(constants.shape, bf16),
            pltpu.VMEM((SEC + 1, WIDE, COLS), bf16),
            pltpu.VMEM((SEC + 1, WIDE, COLS), bf16),
            pltpu.VMEM((SEC + 1, 4 * PATCH, COLS), bf16),
            pltpu.VMEM((2 * SEC, 4 * HALF, COLS), f32),
            pltpu.VMEM((NODES, 4 * HALF, COLS), f32),
            pltpu.VMEM((NODES, 2 * SEC, NODES * LANES), f32),
            pltpu.VMEM((NODES, 2 * SEC, NODES * LANES), f32),
            pltpu.VMEM((1, 2, LANES), f32),
            pltpu.VMEM(((X_COUNT + 2) * tiles, 2, LANES), f32),
            pltpu.VMEM((z_count, 1, LANES), f32),
            dma((4,)),
            dma((6,)),
            dma((6,)),
            dma((2,)),
            dma,
            dma,
            dma,
        ],
        compiler_params=pltpu.CompilerParams(
            collective_id=0, has_side_effects=True, vmem_limit_bytes=64 * 1024 * 1024 - 65536
        ),
    )(images, tissue_mask, constants)


def solution(mesh):
    placed = (P("slab", "tile", None), P("slab", "tile", None))
    return jax.shard_map(
        functools.partial(local, mesh.shape["slab"], mesh.shape["tile"]),
        mesh=mesh,
        in_specs=placed,
        out_specs=(P(None, "slab", "tile", None), P(None, "slab", "tile", None)),
        check_vma=False,
    )
```

```python
import functools

import jax
import jax.numpy as jnp
import ml_dtypes
import numpy as np
from jax import lax
from jax.experimental import pallas as pl
from jax.experimental.pallas import tpu as pltpu
from jax.sharding import PartitionSpec as P

MESH = pl.DeviceIdType.MESH
PATCH = 128
STRIDE = 64
HALF = 64
RIM = 32
TEMP = 256
STEPS = 4
BLOCK = 16
SPLIT = 160
X_COUNT = 4
COLS = 256
NODES = 4
SEC = 4
ROWS = 256
WIDE = ROWS + 2 * RIM
LANES = 128

inter_stiff = 1.0
plane_stiff = 0.25
step_size = 0.5
norm_eps = 1e-06

f32 = jnp.float32
bf16 = jnp.bfloat16


def pieces(table):
    high = table.astype(np.float32).astype(ml_dtypes.bfloat16)
    low = (table - high.astype(np.float64)).astype(np.float32).astype(ml_dtypes.bfloat16)
    return high, low


def tables():
    k = np.arange(HALF)[:, None]
    x = np.arange(PATCH)[None, :]
    angle = 2.0 * np.pi * ((k * x) % PATCH) / PATCH
    cosine, sine = np.cos(angle), np.sin(angle)
    alternate = np.where(np.arange(PATCH) % 2 == 0, 1.0, -1.0)
    sine[0] = np.where(np.arange(PATCH) % 2 == 0, 1.0, -1.0)
    forward = np.concatenate([cosine, sine], axis=0)
    back = forward.T
    final = forward * (2.0 * np.log2(np.e) / (PATCH * PATCH * TEMP))

    def from_left(table):
        high, low = pieces(table)
        return np.block([[high, high], [low, np.zeros_like(low)]])

    def from_right(table):
        high, low = pieces(table)
        return np.block([[high, low], [high, np.zeros_like(low)]])

    even, odd = np.roll(back, -RIM, axis=0), np.roll(back, RIM, axis=0)
    return np.stack([from_left(forward), from_right(even), from_right(odd), from_left(back), from_right(final)])


def split(x):
    high = x.astype(bf16)
    low = (x - high.astype(f32)).astype(bf16)
    return high, low


def dot(a, b):
    return jnp.dot(a, b, preferred_element_type=f32)


def iota(shape, dim):
    return lax.broadcasted_iota(jnp.int32, shape, dim)


def kernel(
    slabs,
    tiles,
    images,
    mask_in,
    table_in,
    flow_out,
    mesh_out,
    buf,
    mask,
    table,
    x_h,
    x_l,
    y,
    spec,
    first_spec,
    tops,
    sums,
    outbox,
    inbox,
    plane_sum,
    local_sem,
    img_send,
    img_recv,
    flow_send,
    flow_recv,
    sum_send,
    sum_recv,
    relay,
):
    z_count = max(slabs // X_COUNT, 1)
    plane = X_COUNT * tiles
    p = lax.axis_index("slab")
    t = lax.axis_index("tile")
    p_next, p_back = lax.rem(p + 1, slabs), lax.rem(p + slabs - 1, slabs)
    t_next, t_back = lax.rem(t + 1, tiles), lax.rem(t + tiles - 1, tiles)
    px, pz = lax.rem(p, X_COUNT), lax.div(p, X_COUNT)
    z_next, z_back = lax.rem(pz + 1, z_count), lax.rem(pz + z_count - 1, z_count)
    at_low, at_high = px == 0, px == X_COUNT - 1

    x_ring = [lax.rem(px + a, X_COUNT) for a in range(X_COUNT)]
    t_ring = [lax.rem(t + b, tiles) for b in range(tiles)]
    z_ring = [lax.rem(pz + a, z_count) for a in range(z_count)]

    def hops(step, size):
        return min(step, size - step)

    steps = [(a, b) for a in range(X_COUNT) for b in range(tiles) if a or b]
    steps.sort(key=lambda ab: -hops(ab[0], X_COUNT) - hops(ab[1], tiles) / 2)
    plane_mates = [(pz * X_COUNT + x_ring[a], t_ring[b]) for a, b in steps]
    z_by_step = [(z_ring[n] * X_COUNT + px, t) for n in range(z_count)]
    near_z = [z_by_step[1 % z_count], z_by_step[z_count - 1]]
    reaches = []
    while 2 ** len(reaches) < z_count // 2:
        reaches.append(2 ** len(reaches))

    def tell(n):
        if n < len(reaches):
            for step in (reaches[n], z_count - reaches[n]):
                pl.semaphore_signal(relay.at[n], inc=1, device_id=z_by_step[step], device_id_type=MESH)

    def hear(n):
        if n < len(reaches):
            pl.semaphore_wait(relay.at[n], 2)

    def signal(device):
        pl.semaphore_signal(barrier, inc=1, device_id=device, device_id_type=MESH)

    own = pltpu.make_async_copy(images, buf.at[pl.ds(1, SEC), pl.ds(RIM, ROWS), :], local_sem.at[0])
    first_tables = pltpu.make_async_copy(table_in.at[pl.ds(0, 1)], table.at[pl.ds(0, 1)], local_sem.at[1])
    other_tables = pltpu.make_async_copy(table_in.at[pl.ds(1, 4)], table.at[pl.ds(1, 4)], local_sem.at[2])
    own_mask = pltpu.make_async_copy(mask_in, mask, local_sem.at[3])
    for copy in (own, first_tables, other_tables, own_mask):
        copy.start()

    barrier = pltpu.get_barrier_semaphore()

    for device in near_z:
        signal(device)
    for n in range(tiles):
        signal((z_back * X_COUNT + X_COUNT - 1, n))
        signal((z_next * X_COUNT, n))
    for device in plane_mates:
        signal(device)

    def remote(src, dst, send_sem, recv_sem, device):
        return pltpu.make_async_remote_copy(
            src_ref=src,
            dst_ref=dst,
            send_sem=send_sem,
            recv_sem=recv_sem,
            device_id=device,
            device_id_type=MESH,
        )

    top_rim, bottom_rim = pl.ds(0, RIM), pl.ds(RIM + ROWS, RIM)
    first_rows, last_rows = pl.ds(0, RIM), pl.ds(ROWS - RIM, RIM)
    sections, last, below = pl.ds(1, SEC), pl.ds(SEC - 1, 1), pl.ds(0, 1)
    moves = [
        (images.at[last, pl.ds(0, SPLIT), :], buf.at[below, pl.ds(RIM, SPLIT), :], (p_next, t)),
        (images.at[last, last_rows, :], buf.at[below, top_rim, :], (p_next, t_next)),
        (images.at[last, pl.ds(SPLIT, ROWS - SPLIT), :], buf.at[below, pl.ds(RIM + SPLIT, ROWS - SPLIT), :], (p_next, t)),
        (images.at[last, first_rows, :], buf.at[below, bottom_rim, :], (p_next, t_back)),
        (images.at[:, last_rows, :], buf.at[sections, top_rim, :], (p, t_next)),
        (images.at[:, first_rows, :], buf.at[sections, bottom_rim, :], (p, t_back)),
    ]
    copies = [remote(src, dst, img_send.at[n], img_recv.at[n], device) for n, (src, dst, device) in enumerate(moves)]

    def prepare(s, start, count):
        rows = pl.ds(start, count)
        x_h[s, rows, :], x_l[s, rows, :] = split(buf[s, rows, :])

    def prepare_top(s):
        @pl.when(t == 0)
        def _():
            buf[s, top_rim, :] = jnp.zeros((RIM, COLS), f32)

        prepare(s, 0, RIM)

    def prepare_bottom(s):
        @pl.when(t == tiles - 1)
        def _():
            buf[s, bottom_rim, :] = jnp.zeros((RIM, COLS), f32)

        prepare(s, RIM + ROWS, RIM)

    lane_row = iota((1, LANES), 1)
    left = lane_row < HALF
    special = (lane_row == 0, lane_row == HALF)

    def by_lane(first, second, at_first, at_second):
        value = jnp.where(left, first, second)
        value = jnp.where(special[0], at_first, value)
        return jnp.where(special[1], at_second, value).astype(f32)

    def turn(x):
        return pltpu.roll(x, HALF, 1)

    left_plus = jnp.where(left, 1.0, -1.0).astype(f32)
    to_x = (by_lane(1.0, 1.0, 1.0, 0.0), by_lane(-1.0, 1.0, 0.0, 1.0))
    to_y = (by_lane(1.0, 1.0, 0.0, 1.0), by_lane(1.0, -1.0, 1.0, 0.0))
    to_x_turned, to_y_turned = ([turn(v) for v in pair] for pair in (to_x, to_y))
    to_m = (by_lane(1.0, 1.0, 0.0, 1.0), by_lane(-1.0, -1.0, 1.0, 0.0))
    to_c = (by_lane(1.0, 1.0, 1.0, 0.0), by_lane(1.0, 1.0, 0.0, 0.0), by_lane(0.0, 0.0, 0.0, 1.0))
    to_s = (by_lane(1.0, -1.0, 1.0, 0.0), by_lane(0.0, 0.0, 0.0, -1.0))
    row_zero = iota((8, LANES), 0) == 0
    corner = row_zero & (lax.rem(iota((8, LANES), 1), HALF) == 0)
    lane_tall = iota((PATCH, LANES), 1)
    left_tall = lane_tall < HALF
    lag = iota((PATCH, 1), 0)
    lag = jnp.where(lag < PATCH // 2, lag, lag - PATCH).astype(f32)

    def at_row_zero(value, general):
        return jnp.concatenate([jnp.where(row_zero, value[:8], general[:8]), general[8:]], axis=0)

    def windows(v):
        first, second = v[:, :LANES], v[:, LANES:]
        return [
            jnp.where(lane_tall < LANES - RIM, first, 0.0),
            jnp.where(lane_tall < RIM, second, first),
            jnp.where(lane_tall < LANES - RIM, second, first),
            jnp.where(lane_tall < RIM, 0.0, second),
        ]

    def transform_rows(s, i, place, n):
        rows = pl.ds(pl.multiple_of(i * STRIDE, STRIDE), PATCH)
        window = jnp.concatenate([x_h[s, rows, :], x_l[s, rows, :]], axis=0)
        both = dot(table[0], window)
        for j, part in enumerate(windows(both[:PATCH] + both[PATCH:])):
            start = (n * 2 + j // 2) * PATCH
            y[place, j % 2, start : start + PATCH] = jnp.concatenate(split(part), axis=1)

    def spectra(place):
        both = [dot(y[place, k], table[1 + k]) for k in range(2)]
        both = [x[:, :LANES] + x[:, LANES:] for x in both]
        found = []
        for n in range(2):
            plain, turned = [], []
            for j in range(NODES):
                start = (n * 2 + j // 2) * PATCH
                c, d = both[j % 2][start : start + HALF], both[j % 2][start + HALF : start + PATCH]
                c_turned, d_turned = turn(c), turn(d)
                x_part = at_row_zero(c, c * to_x[0] + d_turned * to_x[1])
                y_part = at_row_zero(d * left_plus, c * to_y[0] + d_turned * to_y[1])
                plain.append(jnp.concatenate([x_part, y_part], axis=0))
                x_part = at_row_zero(c_turned, c_turned * to_x_turned[0] + d * to_x_turned[1])
                y_part = at_row_zero(-d_turned * left_plus, c_turned * to_y_turned[0] + d * to_y_turned[1])
                turned.append(jnp.concatenate([x_part, y_part], axis=0))
            found.append((plain, turned))
        return found

    def keep(ref, index, found):
        for n, parts in enumerate(found):
            for j, part in enumerate(parts):
                ref[index, n, j] = part

    def cross(first, second, j):
        a, a_turned = first[0, j], first[1, j]
        b, b_turned = second[0, j], second[1, j]
        whole = jnp.where(left_tall, a, a_turned) * b + jnp.where(left_tall, a_turned, -a) * b_turned
        alone = 0.5 * a * b
        x = jnp.concatenate([jnp.where(corner, alone[:8], whole[:8]), whole[8:HALF]], axis=0)
        low = whole[HALF:]
        z = jnp.concatenate([jnp.where(corner, alone[HALF : HALF + 8] * left_plus, low[:8]), low[8:]], axis=0)
        m = turn(x * to_m[0] + z * to_m[1])
        cosines = at_row_zero(x, x * to_c[0] + z * to_c[1] + m * to_c[2])
        sines = at_row_zero(z * left_plus, m * to_s[0] + z * to_s[1])
        return split(jnp.concatenate([cosines, sines], axis=0))

    def correlate(first, second):
        out = []
        for j in range(0, NODES, 2):
            parts = [cross(first, second, j + k) for k in range(2)]
            window = jnp.concatenate([jnp.concatenate([part[h] for part in parts], axis=1) for h in range(2)], axis=0)
            both = dot(table[3], window)
            high, low = split(both[:PATCH] + both[PATCH:])
            for k in range(2):
                lanes = slice(k * LANES, (k + 1) * LANES)
                out.append(jnp.concatenate([high[:, lanes], low[:, lanes]], axis=1))
        return out

    def pairs(earlier, rows, firsts, seconds):
        parts = [part for first, second in zip(firsts, seconds) for part in correlate(first, second)]
        both = dot(jnp.concatenate(parts, axis=0), table[4])
        both = both[:, :LANES] + both[:, LANES:]
        for n in range(NODES * len(rows)):
            i, j = rows[n // NODES], n % NODES
            scores = both[n * PATCH : (n + 1) * PATCH]
            top = jnp.max(scores, axis=0, keepdims=True)
            weights = jnp.exp2(scores - top)
            total = jnp.sum(weights, axis=0, keepdims=True)
            moment = jnp.sum(weights * lag, axis=0, keepdims=True)
            place = slice(j * LANES, (j + 1) * LANES)
            tops[i, pl.ds(earlier, 1), place] = top
            tops[i, pl.ds(earlier + SEC, 1), place] = top
            sums[i, pl.ds(earlier, 1), place] = total
            sums[i, pl.ds(earlier + SEC, 1), place] = moment

    def begin():
        pl.semaphore_wait(barrier, plane - 1 + 2 + plane * jnp.where(at_low | at_high, 1, 0))
        for copy in copies:
            copy.start()
        tell(0)

    own.wait()
    for s in range(1, SEC + 1):
        prepare(s, RIM, ROWS)
    first_tables.wait()
    for s in range(1, SEC + 1):
        for n in range(2):
            transform_rows(s, 1 + n, s, n)
    begin()
    other_tables.wait()

    @pl.loop(0, 2)
    def _(outer):
        rows = (1 - outer, 2 + outer)

        @pl.when(outer == 1)
        def _():
            hear(0)
            tell(1)
            for copy in copies[4:]:
                copy.wait_recv()
            for s in range(1, SEC + 1):
                prepare_top(s)
                prepare_bottom(s)
            for s in range(1, SEC + 1):
                for n in range(2):
                    transform_rows(s, 3 * n, s, n)

        for s in range(1, SEC + 1):
            for n, parts in enumerate(spectra(s)):
                if s == 1:
                    keep(first_spec, rows[n], parts)
                keep(spec, (s - 1) * 2 + n, parts)
            if s > 1:
                pairs(s - 1, rows, [spec.at[(s - 2) * 2 + n] for n in range(2)], [spec.at[(s - 1) * 2 + n] for n in range(2)])

    hear(1)
    tell(2)
    for n in range(2):
        for copy in copies[2 * n : 2 * n + 2]:
            copy.wait_recv()
        if n == 0:
            prepare_top(0)
            prepare(0, RIM, SPLIT)
        else:
            prepare(0, RIM + SPLIT, ROWS - SPLIT)
            prepare_bottom(0)
        rows = (2 * n, 2 * n + 1)
        for k in range(2):
            transform_rows(0, rows[k], n, k)
        for k, parts in enumerate(spectra(n)):
            keep(spec, rows[k], parts)
        pairs(0, rows, [spec.at[i] for i in rows], [first_spec.at[i] for i in rows])

    lane8 = iota((8, LANES), 1)
    row8 = iota((8, LANES), 0)
    lag_cols = jnp.where(lane8 < PATCH // 2, lane8, lane8 - PATCH).astype(f32)
    along = jnp.zeros((8, LANES), f32)
    across = jnp.zeros((8, LANES), f32)
    for i in range(NODES):
        for j in range(NODES):
            lanes = slice(j * LANES, (j + 1) * LANES)
            top = tops[i, :, lanes]
            scaled = sums[i, :, lanes] * jnp.exp2(top - jnp.max(top, axis=1, keepdims=True))
            here = lane8 == i * NODES + j
            along = jnp.where(here, jnp.sum(scaled, axis=1, keepdims=True), along)
            across = jnp.where(here, jnp.sum(scaled * lag_cols, axis=1, keepdims=True), across)
    live = lax.rem(row8, SEC) + p > 0
    low_half = row8 < SEC
    numerator = jnp.where(low_half, pltpu.roll(along, SEC, 0), pltpu.roll(across, SEC, 0))
    denominator = jnp.where(low_half, along, pltpu.roll(along, SEC, 0))
    flows = jnp.where(live & (lane8 < BLOCK), numerator / denominator, 0.0)

    own_mask.wait()
    springs = jnp.zeros((8, LANES), f32)
    for i in range(NODES):
        here = jnp.concatenate([mask[s, i : i + 1, :] for s in range(SEC)], axis=0).astype(f32)
        here = jnp.concatenate([here, jnp.zeros((SEC, LANES - NODES), f32)], axis=1)
        here = jnp.concatenate([here, jnp.zeros((SEC, LANES), f32)], axis=0)
        springs = springs + (pltpu.roll(here, i * NODES, 1) if i else here)
    springs = jnp.where(live, springs, 0.0)

    def flat(x):
        return jnp.sum(pltpu.roll(x, 0, 1, stride=BLOCK, stride_axis=0), axis=0, keepdims=True)

    outbox[0, 0:1, :] = flat(flows)
    outbox[0, 1:2, :] = flat(springs)
    inbox[(1 + px) * tiles + t] = outbox[0]

    def give(q, sem, device):
        return remote(outbox, inbox.at[pl.ds(q * tiles + t, 1)], flow_send.at[sem], flow_recv, device)

    def whole(ref, count, sem):
        slots = ref.at[pl.ds(0, count)]
        pltpu.make_async_copy(slots, slots, sem).wait()

    def write(out, x):
        for i in range(NODES):
            moved = pltpu.roll(x, LANES - i * NODES, 1) if i else x
            for c in range(2):
                for s in range(SEC):
                    out[c, s, i : i + 1, :] = moved[c * SEC + s : c * SEC + s + 1, :NODES]

    @pl.when(at_high)
    def _():
        for x in range(X_COUNT):
            for n in range(tiles):
                give(0, 1, (z_next * X_COUNT + x, n)).start()

    @pl.when(at_low)
    def _():
        for x in range(X_COUNT):
            for n in range(tiles):
                give(X_COUNT + 1, 1, (z_back * X_COUNT + x, n)).start()

    for device in plane_mates:
        give(1 + px, 0, device).start()

    write(flow_out, flows)

    whole(inbox, plane - 1 + 2 * tiles, flow_recv)

    block = lax.div(lane8, BLOCK)

    def transpose_blocks(x):
        for bit in (1, 2, 4):
            row_bit, lane_bit = (row8 & bit) > 0, (block & bit) > 0
            up = pltpu.roll(pltpu.roll(x, 8 - bit, 0), BLOCK * bit, 1)
            down = pltpu.roll(pltpu.roll(x, bit, 0), LANES - BLOCK * bit, 1)
            x = jnp.where(row_bit == lane_bit, x, jnp.where(row_bit, down, up))
        return x

    flow_parts, spring_parts = [], []
    for q in range(X_COUNT + 2):
        there = 1.0
        if q == 0:
            there = (pz > 0).astype(f32)
        elif q == X_COUNT + 1:
            there = (pz < z_count - 1).astype(f32)
        here = slice(q * tiles, (q + 1) * tiles)
        flow_q, spring_q = inbox[here, 0, :], inbox[here, 1, :]
        if tiles < 8:
            pad = jnp.zeros((8 - tiles, LANES), f32)
            flow_q, spring_q = (jnp.concatenate([v, pad], axis=0) for v in (flow_q, spring_q))
        flow_parts.append(there * transpose_blocks(flow_q))
        spring_parts.append(there * transpose_blocks(spring_q)[:SEC])
    wide = (X_COUNT + 2) * SEC
    spring = jnp.concatenate(spring_parts, axis=0)
    flow = [jnp.concatenate([v[c * SEC : (c + 1) * SEC] for v in flow_parts], axis=0) for c in range(2)]
    lane = iota((wide, LANES), 1)
    node_col = lax.rem(lane, NODES)
    live_lanes = (lane < tiles * BLOCK).astype(f32)
    has_up, has_down = (lane >= NODES).astype(f32), (lane < LANES - NODES).astype(f32)
    has_left, has_right = (node_col > 0).astype(f32), (node_col < NODES - 1).astype(f32)

    def differ(stretch):
        return inter_stiff * (pltpu.roll(stretch, wide - 1, 0) - stretch)

    def apply(v):
        stretch = spring * (v - pltpu.roll(v, 1, 0))
        beside = (
            has_up * pltpu.roll(v, NODES, 1)
            + has_down * pltpu.roll(v, LANES - NODES, 1)
            + has_left * pltpu.roll(v, 1, 1)
            + has_right * pltpu.roll(v, LANES - 1, 1)
        )
        return live_lanes * (differ(stretch) + plane_stiff * (beside - 4.0 * v))

    powers = []
    for c in range(2):
        chain = [differ(-spring * flow[c])]
        for _ in range(STEPS - 1):
            chain.append(apply(chain[-1]))
        powers.append(chain)
    grams = [(a, b) for a in range(STEPS) for b in range(a, STEPS)]
    core = slice(SEC, SEC + X_COUNT * SEC)
    rows = [
        jnp.sum(powers[0][a][core] * powers[0][b][core] + powers[1][a][core] * powers[1][b][core], axis=0, keepdims=True)
        for a, b in grams
    ]
    totals = jnp.concatenate(rows + [jnp.zeros((16 - len(grams), LANES), f32)], axis=0)
    totals = jnp.sum(totals, axis=1, keepdims=True)
    diagonal = iota((16, LANES), 0) == iota((16, LANES), 1)
    plane_sum[0] = jnp.sum(jnp.where(diagonal, totals, 0.0), axis=0, keepdims=True)

    def to_z(n):
        slot = pl.ds(n, 1)
        return remote(plane_sum.at[pl.ds(0, 1)], plane_sum.at[slot], sum_send, sum_recv, z_by_step[n])

    hear(2)
    for n in sorted(range(1, z_count), key=lambda n: -hops(n, z_count)):
        to_z(n).start()

    mine = []
    for a in range(STEPS):
        both = jnp.zeros((8, LANES), f32)
        for q in range(X_COUNT):
            part = slice(SEC + q * SEC, 2 * SEC + q * SEC)
            here = jnp.concatenate([powers[0][a][part], powers[1][a][part]], axis=0)
            both = jnp.where(px == q, here, both)
        mine.append(pltpu.roll(both, lax.rem(LANES - t * BLOCK, LANES), 1))

    for copy in copies:
        copy.wait_send()

    whole(inbox, plane - 1, flow_send.at[0])

    @pl.when(at_low | at_high)
    def _():
        whole(inbox, plane, flow_send.at[1])

    whole(plane_sum, z_count - 1, sum_recv)

    totals = jnp.sum(plane_sum[0:z_count, 0, :], axis=0, keepdims=True)
    gram = {}
    for n, (a, b) in enumerate(grams):
        gram[a, b] = gram[b, a] = totals[:, n : n + 1]
    count = 2 * SEC * NODES * NODES * slabs * tiles
    zero = jnp.zeros((1, 1), f32)
    force = [zero + 1.0, zero, zero, zero]
    moved = [zero] * STEPS
    for step in range(STEPS):
        square = zero
        for a in range(step + 1):
            square = square + force[a] * force[a] * gram[a, a]
            for b in range(a + 1, step + 1):
                square = square + 2.0 * force[a] * force[b] * gram[a, b]
        scale = step_size / jnp.sqrt(jnp.maximum(square, 0.0) / count + norm_eps)
        moved = [m + scale * f for m, f in zip(moved, force)]
        force = [f + (scale * force[n - 1] if n else 0.0) for n, f in enumerate(force)]
    write(mesh_out, sum(m * v for m, v in zip(moved, mine)))
    whole(plane_sum, z_count - 1, sum_send)


def local(slabs, tiles, images, tissue_mask):
    z_count = max(slabs // X_COUNT, 1)
    plane = X_COUNT * tiles
    vmem = pl.BlockSpec(memory_space=pltpu.VMEM)
    hbm = pl.BlockSpec(memory_space=pltpu.HBM)
    constants = jnp.asarray(tables())
    out = jax.ShapeDtypeStruct((2, SEC, NODES, NODES), f32)
    dma = pltpu.SemaphoreType.DMA
    return pl.pallas_call(
        functools.partial(kernel, slabs, tiles),
        out_shape=(out, out),
        in_specs=[hbm, hbm, hbm],
        out_specs=(vmem, vmem),
        scratch_shapes=[
            pltpu.VMEM((SEC + 1, WIDE, COLS), f32),
            pltpu.VMEM((SEC, NODES, NODES), jnp.int32),
            pltpu.VMEM(constants.shape, bf16),
            pltpu.VMEM((SEC + 1, WIDE, COLS), bf16),
            pltpu.VMEM((SEC + 1, WIDE, COLS), bf16),
            pltpu.VMEM((SEC + 1, 2, NODES * PATCH, COLS), bf16),
            pltpu.VMEM((2 * SEC, 2, NODES, PATCH, LANES), f32),
            pltpu.VMEM((NODES, 2, NODES, PATCH, LANES), f32),
            pltpu.VMEM((NODES, 2 * SEC, NODES * LANES), f32),
            pltpu.VMEM((NODES, 2 * SEC, NODES * LANES), f32),
            pltpu.VMEM((1, 2, LANES), f32),
            pltpu.VMEM(((X_COUNT + 2) * tiles, 2, LANES), f32),
            pltpu.VMEM((z_count, 1, LANES), f32),
            dma((4,)),
            dma((6,)),
            dma((6,)),
            dma((2,)),
            dma,
            dma,
            dma,
            pltpu.SemaphoreType.REGULAR((3,)),
        ],
        compiler_params=pltpu.CompilerParams(
            collective_id=0, has_side_effects=True, vmem_limit_bytes=64 * 1024 * 1024 - 65536
        ),
    )(images, tissue_mask, constants)


def solution(mesh):
    placed = (P("slab", "tile", None), P("slab", "tile", None))
    return jax.shard_map(
        functools.partial(local, mesh.shape["slab"], mesh.shape["tile"]),
        mesh=mesh,
        in_specs=placed,
        out_specs=(P(None, "slab", "tile", None), P(None, "slab", "tile", None)),
        check_vma=False,
    )
```

```python
import functools

import jax
import jax.numpy as jnp
import ml_dtypes
import numpy as np
from jax import lax
from jax.experimental import pallas as pl
from jax.experimental.pallas import tpu as pltpu
from jax.sharding import PartitionSpec as P

MESH = pl.DeviceIdType.MESH
PATCH = 128
STRIDE = 64
HALF = 64
RIM = 32
TEMP = 256
STEPS = 4
BLOCK = 16
SPLIT = 160
X_COUNT = 4
COLS = 256
NODES = 4
SEC = 4
ROWS = 256
WIDE = ROWS + 2 * RIM
LANES = 128

inter_stiff = 1.0
plane_stiff = 0.25
step_size = 0.5
norm_eps = 1e-06

f32 = jnp.float32
bf16 = jnp.bfloat16


def pieces(table):
    high = table.astype(np.float32).astype(ml_dtypes.bfloat16)
    low = (table - high.astype(np.float64)).astype(np.float32).astype(ml_dtypes.bfloat16)
    return high, low


def tables():
    k = np.arange(HALF)[:, None]
    x = np.arange(PATCH)[None, :]
    angle = 2.0 * np.pi * ((k * x) % PATCH) / PATCH
    cosine, sine = np.cos(angle), np.sin(angle)
    alternate = np.where(np.arange(PATCH) % 2 == 0, 1.0, -1.0)
    sine[0] = np.where(np.arange(PATCH) % 2 == 0, 1.0, -1.0)
    forward = np.concatenate([cosine, sine], axis=0)
    back = forward.T
    final = forward * (2.0 * np.log2(np.e) / (PATCH * PATCH * TEMP))

    def from_left(table):
        high, low = pieces(table)
        return np.block([[high, high], [low, np.zeros_like(low)]])

    def from_right(table):
        high, low = pieces(table)
        return np.block([[high, low], [high, np.zeros_like(low)]])

    even, odd = np.roll(back, -RIM, axis=0), np.roll(back, RIM, axis=0)
    return np.stack([from_left(forward), from_right(even), from_right(odd), from_left(back), from_right(final)])


def split(x):
    high = x.astype(bf16)
    low = (x - high.astype(f32)).astype(bf16)
    return high, low


def dot(a, b):
    return jnp.dot(a, b, preferred_element_type=f32)


def iota(shape, dim):
    return lax.broadcasted_iota(jnp.int32, shape, dim)


def kernel(
    slabs,
    tiles,
    images,
    mask_in,
    table_in,
    flow_out,
    mesh_out,
    buf,
    mask,
    table,
    x_h,
    x_l,
    y,
    spec,
    first_spec,
    tops,
    sums,
    outbox,
    inbox,
    plane_sum,
    local_sem,
    img_send,
    img_recv,
    flow_send,
    flow_recv,
    sum_send,
    sum_recv,
    relay,
):
    z_count = max(slabs // X_COUNT, 1)
    plane = X_COUNT * tiles
    p = lax.axis_index("slab")
    t = lax.axis_index("tile")
    p_next, p_back = lax.rem(p + 1, slabs), lax.rem(p + slabs - 1, slabs)
    t_next, t_back = lax.rem(t + 1, tiles), lax.rem(t + tiles - 1, tiles)
    px, pz = lax.rem(p, X_COUNT), lax.div(p, X_COUNT)
    z_next, z_back = lax.rem(pz + 1, z_count), lax.rem(pz + z_count - 1, z_count)
    at_low, at_high = px == 0, px == X_COUNT - 1

    x_ring = [lax.rem(px + a, X_COUNT) for a in range(X_COUNT)]
    t_ring = [lax.rem(t + b, tiles) for b in range(tiles)]
    z_ring = [lax.rem(pz + a, z_count) for a in range(z_count)]

    def hops(step, size):
        return min(step, size - step)

    steps = [(a, b) for a in range(X_COUNT) for b in range(tiles) if a or b]
    steps.sort(key=lambda ab: -hops(ab[0], X_COUNT) - hops(ab[1], tiles) / 2)
    plane_mates = [(pz * X_COUNT + x_ring[a], t_ring[b]) for a, b in steps]
    z_by_step = [(z_ring[n] * X_COUNT + px, t) for n in range(z_count)]
    near = [(a, b) for a in (p_back, p, p_next) for b in (t_back, t, t_next)]
    near.pop(4)
    near += [z_by_step[1 % z_count], z_by_step[z_count - 1]]
    p_ring = (lax.rem(p + slabs - 2, slabs), p, lax.rem(p + 2, slabs))
    t_wide = (lax.rem(t + tiles - 2, tiles), t, lax.rem(t + 2, tiles))
    wider = [(a, b) for a in p_ring for b in t_wide]
    wider.pop(4)
    wider += [z_by_step[2 % z_count], z_by_step[z_count - 2]]
    rounds = [near, wider, [z_by_step[4 % z_count], z_by_step[z_count - 4]]]

    def tell(n):
        for device in rounds[n]:
            pl.semaphore_signal(relay.at[n], inc=1, device_id=device, device_id_type=MESH)

    def hear(n):
        pl.semaphore_wait(relay.at[n], len(rounds[n]))

    def signal(device):
        pl.semaphore_signal(barrier, inc=1, device_id=device, device_id_type=MESH)

    own = pltpu.make_async_copy(images, buf.at[pl.ds(1, SEC), pl.ds(RIM, ROWS), :], local_sem.at[0])
    first_tables = pltpu.make_async_copy(table_in.at[pl.ds(0, 1)], table.at[pl.ds(0, 1)], local_sem.at[1])
    other_tables = pltpu.make_async_copy(table_in.at[pl.ds(1, 4)], table.at[pl.ds(1, 4)], local_sem.at[2])
    own_mask = pltpu.make_async_copy(mask_in, mask, local_sem.at[3])
    for copy in (own, first_tables, other_tables, own_mask):
        copy.start()

    barrier = pltpu.get_barrier_semaphore()

    for device in near:
        signal(device)

    def remote(src, dst, send_sem, recv_sem, device):
        return pltpu.make_async_remote_copy(
            src_ref=src,
            dst_ref=dst,
            send_sem=send_sem,
            recv_sem=recv_sem,
            device_id=device,
            device_id_type=MESH,
        )

    top_rim, bottom_rim = pl.ds(0, RIM), pl.ds(RIM + ROWS, RIM)
    first_rows, last_rows = pl.ds(0, RIM), pl.ds(ROWS - RIM, RIM)
    sections, last, below = pl.ds(1, SEC), pl.ds(SEC - 1, 1), pl.ds(0, 1)
    moves = [
        (images.at[last, pl.ds(0, SPLIT), :], buf.at[below, pl.ds(RIM, SPLIT), :], (p_next, t)),
        (images.at[last, last_rows, :], buf.at[below, top_rim, :], (p_next, t_next)),
        (images.at[last, pl.ds(SPLIT, ROWS - SPLIT), :], buf.at[below, pl.ds(RIM + SPLIT, ROWS - SPLIT), :], (p_next, t)),
        (images.at[last, first_rows, :], buf.at[below, bottom_rim, :], (p_next, t_back)),
        (images.at[:, last_rows, :], buf.at[sections, top_rim, :], (p, t_next)),
        (images.at[:, first_rows, :], buf.at[sections, bottom_rim, :], (p, t_back)),
    ]
    copies = [remote(src, dst, img_send.at[n], img_recv.at[n], device) for n, (src, dst, device) in enumerate(moves)]

    def prepare(s, start, count):
        rows = pl.ds(start, count)
        x_h[s, rows, :], x_l[s, rows, :] = split(buf[s, rows, :])

    def prepare_top(s):
        @pl.when(t == 0)
        def _():
            buf[s, top_rim, :] = jnp.zeros((RIM, COLS), f32)

        prepare(s, 0, RIM)

    def prepare_bottom(s):
        @pl.when(t == tiles - 1)
        def _():
            buf[s, bottom_rim, :] = jnp.zeros((RIM, COLS), f32)

        prepare(s, RIM + ROWS, RIM)

    lane_row = iota((1, LANES), 1)
    left = lane_row < HALF
    special = (lane_row == 0, lane_row == HALF)

    def by_lane(first, second, at_first, at_second):
        value = jnp.where(left, first, second)
        value = jnp.where(special[0], at_first, value)
        return jnp.where(special[1], at_second, value).astype(f32)

    def turn(x):
        return pltpu.roll(x, HALF, 1)

    left_plus = jnp.where(left, 1.0, -1.0).astype(f32)
    to_x = (by_lane(1.0, 1.0, 1.0, 0.0), by_lane(-1.0, 1.0, 0.0, 1.0))
    to_y = (by_lane(1.0, 1.0, 0.0, 1.0), by_lane(1.0, -1.0, 1.0, 0.0))
    to_x_turned, to_y_turned = ([turn(v) for v in pair] for pair in (to_x, to_y))
    to_m = (by_lane(1.0, 1.0, 0.0, 1.0), by_lane(-1.0, -1.0, 1.0, 0.0))
    to_c = (by_lane(1.0, 1.0, 1.0, 0.0), by_lane(1.0, 1.0, 0.0, 0.0), by_lane(0.0, 0.0, 0.0, 1.0))
    to_s = (by_lane(1.0, -1.0, 1.0, 0.0), by_lane(0.0, 0.0, 0.0, -1.0))
    row_zero = iota((8, LANES), 0) == 0
    corner = row_zero & (lax.rem(iota((8, LANES), 1), HALF) == 0)
    lane_tall = iota((PATCH, LANES), 1)
    left_tall = lane_tall < HALF
    lag = iota((PATCH, 1), 0)
    lag = jnp.where(lag < PATCH // 2, lag, lag - PATCH).astype(f32)

    def at_row_zero(value, general):
        return jnp.concatenate([jnp.where(row_zero, value[:8], general[:8]), general[8:]], axis=0)

    def windows(v):
        first, second = v[:, :LANES], v[:, LANES:]
        return [
            jnp.where(lane_tall < LANES - RIM, first, 0.0),
            jnp.where(lane_tall < RIM, second, first),
            jnp.where(lane_tall < LANES - RIM, second, first),
            jnp.where(lane_tall < RIM, 0.0, second),
        ]

    def transform_rows(s, i, place, n):
        rows = pl.ds(pl.multiple_of(i * STRIDE, STRIDE), PATCH)
        window = jnp.concatenate([x_h[s, rows, :], x_l[s, rows, :]], axis=0)
        both = dot(table[0], window)
        for j, part in enumerate(windows(both[:PATCH] + both[PATCH:])):
            start = (n * 2 + j // 2) * PATCH
            y[place, j % 2, start : start + PATCH] = jnp.concatenate(split(part), axis=1)

    def spectra(place):
        both = [dot(y[place, k], table[1 + k]) for k in range(2)]
        both = [x[:, :LANES] + x[:, LANES:] for x in both]
        found = []
        for n in range(2):
            plain, turned = [], []
            for j in range(NODES):
                start = (n * 2 + j // 2) * PATCH
                c, d = both[j % 2][start : start + HALF], both[j % 2][start + HALF : start + PATCH]
                c_turned, d_turned = turn(c), turn(d)
                x_part = at_row_zero(c, c * to_x[0] + d_turned * to_x[1])
                y_part = at_row_zero(d * left_plus, c * to_y[0] + d_turned * to_y[1])
                plain.append(jnp.concatenate([x_part, y_part], axis=0))
                x_part = at_row_zero(c_turned, c_turned * to_x_turned[0] + d * to_x_turned[1])
                y_part = at_row_zero(-d_turned * left_plus, c_turned * to_y_turned[0] + d * to_y_turned[1])
                turned.append(jnp.concatenate([x_part, y_part], axis=0))
            found.append((plain, turned))
        return found

    def keep(ref, index, found):
        for n, parts in enumerate(found):
            for j, part in enumerate(parts):
                ref[index, n, j] = part

    def cross(first, second, j):
        a, a_turned = first[0, j], first[1, j]
        b, b_turned = second[0, j], second[1, j]
        whole = jnp.where(left_tall, a, a_turned) * b + jnp.where(left_tall, a_turned, -a) * b_turned
        alone = 0.5 * a * b
        x = jnp.concatenate([jnp.where(corner, alone[:8], whole[:8]), whole[8:HALF]], axis=0)
        low = whole[HALF:]
        z = jnp.concatenate([jnp.where(corner, alone[HALF : HALF + 8] * left_plus, low[:8]), low[8:]], axis=0)
        m = turn(x * to_m[0] + z * to_m[1])
        cosines = at_row_zero(x, x * to_c[0] + z * to_c[1] + m * to_c[2])
        sines = at_row_zero(z * left_plus, m * to_s[0] + z * to_s[1])
        return split(jnp.concatenate([cosines, sines], axis=0))

    def correlate(first, second):
        out = []
        for j in range(0, NODES, 2):
            parts = [cross(first, second, j + k) for k in range(2)]
            window = jnp.concatenate([jnp.concatenate([part[h] for part in parts], axis=1) for h in range(2)], axis=0)
            both = dot(table[3], window)
            high, low = split(both[:PATCH] + both[PATCH:])
            for k in range(2):
                lanes = slice(k * LANES, (k + 1) * LANES)
                out.append(jnp.concatenate([high[:, lanes], low[:, lanes]], axis=1))
        return out

    def pairs(earlier, rows, firsts, seconds):
        parts = [part for first, second in zip(firsts, seconds) for part in correlate(first, second)]
        both = dot(jnp.concatenate(parts, axis=0), table[4])
        both = both[:, :LANES] + both[:, LANES:]
        for n in range(NODES * len(rows)):
            i, j = rows[n // NODES], n % NODES
            scores = both[n * PATCH : (n + 1) * PATCH]
            top = jnp.max(scores, axis=0, keepdims=True)
            weights = jnp.exp2(scores - top)
            total = jnp.sum(weights, axis=0, keepdims=True)
            moment = jnp.sum(weights * lag, axis=0, keepdims=True)
            place = slice(j * LANES, (j + 1) * LANES)
            tops[i, pl.ds(earlier, 1), place] = top
            tops[i, pl.ds(earlier + SEC, 1), place] = top
            sums[i, pl.ds(earlier, 1), place] = total
            sums[i, pl.ds(earlier + SEC, 1), place] = moment

    def begin():
        pl.semaphore_wait(barrier, len(near))
        for copy in copies:
            copy.start()
        tell(0)

    lane8 = iota((8, LANES), 1)
    row8 = iota((8, LANES), 0)
    live = lax.rem(row8, SEC) + p > 0
    own_mask.wait()
    springs = jnp.zeros((8, LANES), f32)
    for i in range(NODES):
        here = jnp.concatenate([mask[s, i : i + 1, :] for s in range(SEC)], axis=0).astype(f32)
        here = jnp.concatenate([here, jnp.zeros((SEC, LANES - NODES), f32)], axis=1)
        here = jnp.concatenate([here, jnp.zeros((SEC, LANES), f32)], axis=0)
        springs = springs + (pltpu.roll(here, i * NODES, 1) if i else here)
    springs = jnp.where(live, springs, 0.0)

    def flat(x):
        return jnp.sum(pltpu.roll(x, 0, 1, stride=BLOCK, stride_axis=0), axis=0, keepdims=True)

    outbox[0, 1:2, :] = flat(springs)
    own.wait()
    for s in range(1, SEC + 1):
        prepare(s, RIM, ROWS)
    first_tables.wait()
    for s in range(1, SEC + 1):
        for n in range(2):
            transform_rows(s, 1 + n, s, n)
    begin()
    other_tables.wait()

    @pl.loop(0, 2)
    def _(outer):
        rows = (1 - outer, 2 + outer)

        @pl.when(outer == 1)
        def _():
            hear(0)
            tell(1)
            for copy in copies[4:]:
                copy.wait_recv()
            for s in range(1, SEC + 1):
                prepare_top(s)
                prepare_bottom(s)
            for s in range(1, SEC + 1):
                for n in range(2):
                    transform_rows(s, 3 * n, s, n)

        for s in range(1, SEC + 1):
            for n, parts in enumerate(spectra(s)):
                if s == 1:
                    keep(first_spec, rows[n], parts)
                keep(spec, (s - 1) * 2 + n, parts)
            if s > 1:
                pairs(s - 1, rows, [spec.at[(s - 2) * 2 + n] for n in range(2)], [spec.at[(s - 1) * 2 + n] for n in range(2)])

    hear(1)
    tell(2)
    for n in range(2):
        for copy in copies[2 * n : 2 * n + 2]:
            copy.wait_recv()
        if n == 0:
            prepare_top(0)
            prepare(0, RIM, SPLIT)
        else:
            prepare(0, RIM + SPLIT, ROWS - SPLIT)
            prepare_bottom(0)
        rows = (2 * n, 2 * n + 1)
        for k in range(2):
            transform_rows(0, rows[k], n, k)
        for k, parts in enumerate(spectra(n)):
            keep(spec, rows[k], parts)
        pairs(0, rows, [spec.at[i] for i in rows], [first_spec.at[i] for i in rows])

    lag_cols = jnp.where(lane8 < PATCH // 2, lane8, lane8 - PATCH).astype(f32)
    along = jnp.zeros((8, LANES), f32)
    across = jnp.zeros((8, LANES), f32)
    for i in range(NODES):
        for j in range(NODES):
            lanes = slice(j * LANES, (j + 1) * LANES)
            top = tops[i, :, lanes]
            scaled = sums[i, :, lanes] * jnp.exp2(top - jnp.max(top, axis=1, keepdims=True))
            here = lane8 == i * NODES + j
            along = jnp.where(here, jnp.sum(scaled, axis=1, keepdims=True), along)
            across = jnp.where(here, jnp.sum(scaled * lag_cols, axis=1, keepdims=True), across)
    low_half = row8 < SEC
    numerator = jnp.where(low_half, pltpu.roll(along, SEC, 0), pltpu.roll(across, SEC, 0))
    denominator = jnp.where(low_half, along, pltpu.roll(along, SEC, 0))
    flows = jnp.where(live & (lane8 < BLOCK), numerator / denominator, 0.0)

    outbox[0, 0:1, :] = flat(flows)
    inbox[(1 + px) * tiles + t] = outbox[0]

    def give(q, sem, device):
        return remote(outbox, inbox.at[pl.ds(q * tiles + t, 1)], flow_send.at[sem], flow_recv, device)

    def whole(ref, count, sem):
        slots = ref.at[pl.ds(0, count)]
        pltpu.make_async_copy(slots, slots, sem).wait()

    def write(out, x):
        for i in range(NODES):
            moved = pltpu.roll(x, LANES - i * NODES, 1) if i else x
            for c in range(2):
                for s in range(SEC):
                    out[c, s, i : i + 1, :] = moved[c * SEC + s : c * SEC + s + 1, :NODES]

    for device in plane_mates:
        give(1 + px, 0, device).start()

    @pl.when(at_high)
    def _():
        for x in range(X_COUNT):
            for n in range(tiles):
                give(0, 1, (z_next * X_COUNT + x, n)).start()

    @pl.when(at_low)
    def _():
        for x in range(X_COUNT):
            for n in range(tiles):
                give(X_COUNT + 1, 1, (z_back * X_COUNT + x, n)).start()


    write(flow_out, flows)

    whole(inbox, plane - 1 + 2 * tiles, flow_recv)

    block = lax.div(lane8, BLOCK)

    def transpose_blocks(x):
        for bit in (1, 2, 4):
            row_bit, lane_bit = (row8 & bit) > 0, (block & bit) > 0
            up = pltpu.roll(pltpu.roll(x, 8 - bit, 0), BLOCK * bit, 1)
            down = pltpu.roll(pltpu.roll(x, bit, 0), LANES - BLOCK * bit, 1)
            x = jnp.where(row_bit == lane_bit, x, jnp.where(row_bit, down, up))
        return x

    def received(q, row):
        x = inbox[q * tiles : (q + 1) * tiles, row, :]
        if tiles < 8:
            x = jnp.concatenate([x, jnp.zeros((8 - tiles, LANES), f32)], axis=0)
        if q == 0:
            x = x * (pz > 0).astype(f32)
        elif q == X_COUNT + 1:
            x = x * (pz < z_count - 1).astype(f32)
        return x

    flow_parts, spring_parts = ([], []), []
    left8 = lane8 < HALF
    for q in range(0, X_COUNT + 2, 2):
        first, second = received(q, 0), received(q + 1, 0)
        flow_parts[0].append(transpose_blocks(jnp.where(left8, first, pltpu.roll(second, HALF, 1))))
        flow_parts[1].append(transpose_blocks(jnp.where(left8, pltpu.roll(first, HALF, 1), second)))
        spring_parts.append(transpose_blocks(received(q, 1) + pltpu.roll(received(q + 1, 1), HALF, 1)))
    wide = (X_COUNT + 2) * SEC
    spring = jnp.concatenate(spring_parts, axis=0)
    flow = [jnp.concatenate(parts, axis=0) for parts in flow_parts]
    lane = iota((wide, LANES), 1)
    node_col = lax.rem(lane, NODES)
    live_lanes = (lane < tiles * BLOCK).astype(f32)
    has_up, has_down = (lane >= NODES).astype(f32), (lane < LANES - NODES).astype(f32)
    has_left, has_right = (node_col > 0).astype(f32), (node_col < NODES - 1).astype(f32)

    def differ(stretch):
        return inter_stiff * (pltpu.roll(stretch, wide - 1, 0) - stretch)

    def apply(v):
        stretch = spring * (v - pltpu.roll(v, 1, 0))
        beside = (
            has_up * pltpu.roll(v, NODES, 1)
            + has_down * pltpu.roll(v, LANES - NODES, 1)
            + has_left * pltpu.roll(v, 1, 1)
            + has_right * pltpu.roll(v, LANES - 1, 1)
        )
        return live_lanes * (differ(stretch) + plane_stiff * (beside - 4.0 * v))

    powers = []
    for c in range(2):
        chain = [differ(-spring * flow[c])]
        for _ in range(STEPS - 1):
            chain.append(apply(chain[-1]))
        powers.append(chain)
    grams = [(a, b) for a in range(STEPS) for b in range(a, STEPS)]
    row = iota((wide, LANES), 0)
    inner = ((row >= SEC) & (row < wide - SEC)).astype(f32)
    inner_powers = [[v * inner for v in chain] for chain in powers]
    rows = [
        jnp.sum(inner_powers[0][a] * powers[0][b] + inner_powers[1][a] * powers[1][b], axis=0, keepdims=True)
        for a, b in grams
    ]
    totals = jnp.concatenate(rows + [jnp.zeros((16 - len(grams), LANES), f32)], axis=0)
    totals = jnp.sum(totals, axis=1, keepdims=True)
    diagonal = iota((16, LANES), 0) == iota((16, LANES), 1)
    plane_sum[0] = jnp.sum(jnp.where(diagonal, totals, 0.0), axis=0, keepdims=True)

    def to_z(n):
        slot = pl.ds(n, 1)
        return remote(plane_sum.at[pl.ds(0, 1)], plane_sum.at[slot], sum_send, sum_recv, z_by_step[n])

    hear(2)
    for n in sorted(range(1, z_count), key=lambda n: -hops(n, z_count)):
        to_z(n).start()

    mine = []
    for a in range(STEPS):
        both = jnp.zeros((8, LANES), f32)
        for q in range(X_COUNT):
            part = slice(SEC + q * SEC, 2 * SEC + q * SEC)
            here = jnp.concatenate([powers[0][a][part], powers[1][a][part]], axis=0)
            both = jnp.where(px == q, here, both)
        mine.append(pltpu.roll(both, lax.rem(LANES - t * BLOCK, LANES), 1))

    for copy in copies:
        copy.wait_send()

    whole(inbox, plane - 1, flow_send.at[0])

    @pl.when(at_low | at_high)
    def _():
        whole(inbox, plane, flow_send.at[1])

    whole(plane_sum, z_count - 1, sum_recv)

    totals = jnp.sum(plane_sum[0:z_count, 0, :], axis=0, keepdims=True)
    gram = {}
    for n, (a, b) in enumerate(grams):
        gram[a, b] = gram[b, a] = totals[:, n : n + 1]
    count = 2 * SEC * NODES * NODES * slabs * tiles
    zero = jnp.zeros((1, 1), f32)
    force = [zero + 1.0, zero, zero, zero]
    moved = [zero] * STEPS
    for step in range(STEPS):
        square = zero
        for a in range(step + 1):
            square = square + force[a] * force[a] * gram[a, a]
            for b in range(a + 1, step + 1):
                square = square + 2.0 * force[a] * force[b] * gram[a, b]
        scale = step_size / jnp.sqrt(jnp.maximum(square, 0.0) / count + norm_eps)
        moved = [m + scale * f for m, f in zip(moved, force)]
        force = [f + (scale * force[n - 1] if n else 0.0) for n, f in enumerate(force)]
    write(mesh_out, sum(m * v for m, v in zip(moved, mine)))
    whole(plane_sum, z_count - 1, sum_send)


def local(slabs, tiles, images, tissue_mask):
    z_count = max(slabs // X_COUNT, 1)
    plane = X_COUNT * tiles
    vmem = pl.BlockSpec(memory_space=pltpu.VMEM)
    hbm = pl.BlockSpec(memory_space=pltpu.HBM)
    constants = jnp.asarray(tables())
    out = jax.ShapeDtypeStruct((2, SEC, NODES, NODES), f32)
    dma = pltpu.SemaphoreType.DMA
    return pl.pallas_call(
        functools.partial(kernel, slabs, tiles),
        out_shape=(out, out),
        in_specs=[hbm, hbm, hbm],
        out_specs=(vmem, vmem),
        scratch_shapes=[
            pltpu.VMEM((SEC + 1, WIDE, COLS), f32),
            pltpu.VMEM((SEC, NODES, NODES), jnp.int32),
            pltpu.VMEM(constants.shape, bf16),
            pltpu.VMEM((SEC + 1, WIDE, COLS), bf16),
            pltpu.VMEM((SEC + 1, WIDE, COLS), bf16),
            pltpu.VMEM((SEC + 1, 2, NODES * PATCH, COLS), bf16),
            pltpu.VMEM((2 * SEC, 2, NODES, PATCH, LANES), f32),
            pltpu.VMEM((NODES, 2, NODES, PATCH, LANES), f32),
            pltpu.VMEM((NODES, 2 * SEC, NODES * LANES), f32),
            pltpu.VMEM((NODES, 2 * SEC, NODES * LANES), f32),
            pltpu.VMEM((1, 2, LANES), f32),
            pltpu.VMEM(((X_COUNT + 2) * tiles, 2, LANES), f32),
            pltpu.VMEM((z_count, 1, LANES), f32),
            dma((4,)),
            dma((6,)),
            dma((6,)),
            dma((2,)),
            dma,
            dma,
            dma,
            pltpu.SemaphoreType.REGULAR((3,)),
        ],
        compiler_params=pltpu.CompilerParams(
            collective_id=0, has_side_effects=True, vmem_limit_bytes=64 * 1024 * 1024 - 65536
        ),
    )(images, tissue_mask, constants)


def solution(mesh):
    placed = (P("slab", "tile", None), P("slab", "tile", None))
    return jax.shard_map(
        functools.partial(local, mesh.shape["slab"], mesh.shape["tile"]),
        mesh=mesh,
        in_specs=placed,
        out_specs=(P(None, "slab", "tile", None), P(None, "slab", "tile", None)),
        check_vma=False,
    )
```

```python
import functools

import jax
import jax.numpy as jnp
import ml_dtypes
import numpy as np
from jax import lax
from jax.experimental import pallas as pl
from jax.experimental.pallas import tpu as pltpu
from jax.sharding import PartitionSpec as P

MESH = pl.DeviceIdType.MESH
PATCH = 128
STRIDE = 64
HALF = 64
RIM = 32
TEMP = 256
STEPS = 4
BLOCK = 16
SPLIT = 160
X_COUNT = 4
COLS = 256
NODES = 4
SEC = 4
ROWS = 256
WIDE = ROWS + 2 * RIM
LANES = 128

inter_stiff = 1.0
plane_stiff = 0.25
step_size = 0.5
norm_eps = 1e-06

f32 = jnp.float32
bf16 = jnp.bfloat16


def pieces(table):
    high = table.astype(np.float32).astype(ml_dtypes.bfloat16)
    low = (table - high.astype(np.float64)).astype(np.float32).astype(ml_dtypes.bfloat16)
    return high, low


def tables():
    k = np.arange(HALF)[:, None]
    x = np.arange(PATCH)[None, :]
    angle = 2.0 * np.pi * ((k * x) % PATCH) / PATCH
    cosine, sine = np.cos(angle), np.sin(angle)
    alternate = np.where(np.arange(PATCH) % 2 == 0, 1.0, -1.0)
    sine[0] = np.where(np.arange(PATCH) % 2 == 0, 1.0, -1.0)
    forward = np.concatenate([cosine, sine], axis=0)
    back = forward.T
    final = forward * (2.0 * np.log2(np.e) / (PATCH * PATCH * TEMP))

    def from_left(table):
        high, low = pieces(table)
        return np.block([[high, high], [low, np.zeros_like(low)]])

    def from_right(table):
        high, low = pieces(table)
        return np.block([[high, low], [high, np.zeros_like(low)]])

    even, odd = np.roll(back, -RIM, axis=0), np.roll(back, RIM, axis=0)
    return np.stack([from_left(forward), from_right(even), from_right(odd), from_left(back), from_right(final)])


def split(x):
    high = x.astype(bf16)
    low = (x - high.astype(f32)).astype(bf16)
    return high, low


def dot(a, b):
    return jnp.dot(a, b, preferred_element_type=f32)


def iota(shape, dim):
    return lax.broadcasted_iota(jnp.int32, shape, dim)


def kernel(
    slabs,
    tiles,
    images,
    mask_in,
    table_in,
    flow_out,
    mesh_out,
    buf,
    mask,
    table,
    x_h,
    x_l,
    y,
    spec,
    first_spec,
    tops,
    sums,
    outbox,
    inbox,
    plane_sum,
    local_sem,
    img_send,
    img_recv,
    flow_send,
    flow_recv,
    sum_send,
    sum_recv,
    relay,
):
    z_count = max(slabs // X_COUNT, 1)
    plane = X_COUNT * tiles
    p = lax.axis_index("slab")
    t = lax.axis_index("tile")
    p_next, p_back = lax.rem(p + 1, slabs), lax.rem(p + slabs - 1, slabs)
    t_next, t_back = lax.rem(t + 1, tiles), lax.rem(t + tiles - 1, tiles)
    px, pz = lax.rem(p, X_COUNT), lax.div(p, X_COUNT)
    z_next, z_back = lax.rem(pz + 1, z_count), lax.rem(pz + z_count - 1, z_count)
    at_low, at_high = px == 0, px == X_COUNT - 1

    x_ring = [lax.rem(px + a, X_COUNT) for a in range(X_COUNT)]
    t_ring = [lax.rem(t + b, tiles) for b in range(tiles)]
    z_ring = [lax.rem(pz + a, z_count) for a in range(z_count)]

    def hops(step, size):
        return min(step, size - step)

    steps = [(a, b) for a in range(X_COUNT) for b in range(tiles) if a or b]
    steps.sort(key=lambda ab: -hops(ab[0], X_COUNT) - hops(ab[1], tiles) / 2)
    plane_mates = [(pz * X_COUNT + x_ring[a], t_ring[b]) for a, b in steps]
    z_by_step = [(z_ring[n] * X_COUNT + px, t) for n in range(z_count)]
    near = [(a, b) for a in (p_back, p, p_next) for b in (t_back, t, t_next)]
    near.pop(4)
    near += [z_by_step[1 % z_count], z_by_step[z_count - 1]]
    p_ring = (lax.rem(p + slabs - 2, slabs), p, lax.rem(p + 2, slabs))
    t_wide = (lax.rem(t + tiles - 2, tiles), t, lax.rem(t + 2, tiles))
    wider = [(a, b) for a in p_ring for b in t_wide]
    wider.pop(4)
    wider += [z_by_step[2 % z_count], z_by_step[z_count - 2]]
    rounds = [near, wider, [z_by_step[4 % z_count], z_by_step[z_count - 4]]]

    def tell(n):
        for device in rounds[n]:
            pl.semaphore_signal(relay.at[n], inc=1, device_id=device, device_id_type=MESH)

    def hear(n):
        pl.semaphore_wait(relay.at[n], len(rounds[n]))

    def signal(device):
        pl.semaphore_signal(barrier, inc=1, device_id=device, device_id_type=MESH)

    own = pltpu.make_async_copy(images, buf.at[pl.ds(1, SEC), pl.ds(RIM, ROWS), :], local_sem.at[0])
    first_tables = pltpu.make_async_copy(table_in.at[pl.ds(0, 1)], table.at[pl.ds(0, 1)], local_sem.at[1])
    other_tables = pltpu.make_async_copy(table_in.at[pl.ds(1, 4)], table.at[pl.ds(1, 4)], local_sem.at[2])
    own_mask = pltpu.make_async_copy(mask_in, mask, local_sem.at[3])
    for copy in (own, first_tables, other_tables, own_mask):
        copy.start()

    barrier = pltpu.get_barrier_semaphore()

    for device in near:
        signal(device)

    def remote(src, dst, send_sem, recv_sem, device):
        return pltpu.make_async_remote_copy(
            src_ref=src,
            dst_ref=dst,
            send_sem=send_sem,
            recv_sem=recv_sem,
            device_id=device,
            device_id_type=MESH,
        )

    top_rim, bottom_rim = pl.ds(0, RIM), pl.ds(RIM + ROWS, RIM)
    first_rows, last_rows = pl.ds(0, RIM), pl.ds(ROWS - RIM, RIM)
    sections, last, below = pl.ds(1, SEC), pl.ds(SEC - 1, 1), pl.ds(0, 1)
    moves = [
        (images.at[last, pl.ds(0, SPLIT), :], buf.at[below, pl.ds(RIM, SPLIT), :], (p_next, t)),
        (images.at[last, last_rows, :], buf.at[below, top_rim, :], (p_next, t_next)),
        (images.at[last, pl.ds(SPLIT, ROWS - SPLIT), :], buf.at[below, pl.ds(RIM + SPLIT, ROWS - SPLIT), :], (p_next, t)),
        (images.at[last, first_rows, :], buf.at[below, bottom_rim, :], (p_next, t_back)),
        (images.at[:, last_rows, :], buf.at[sections, top_rim, :], (p, t_next)),
        (images.at[:, first_rows, :], buf.at[sections, bottom_rim, :], (p, t_back)),
    ]
    copies = [remote(src, dst, img_send.at[n], img_recv.at[n], device) for n, (src, dst, device) in enumerate(moves)]

    def prepare(s, start, count):
        rows = pl.ds(start, count)
        x_h[s, rows, :], x_l[s, rows, :] = split(buf[s, rows, :])

    def prepare_top(s):
        @pl.when(t == 0)
        def _():
            buf[s, top_rim, :] = jnp.zeros((RIM, COLS), f32)

        prepare(s, 0, RIM)

    def prepare_bottom(s):
        @pl.when(t == tiles - 1)
        def _():
            buf[s, bottom_rim, :] = jnp.zeros((RIM, COLS), f32)

        prepare(s, RIM + ROWS, RIM)

    lane_row = iota((1, LANES), 1)
    left = lane_row < HALF
    special = (lane_row == 0, lane_row == HALF)

    def by_lane(first, second, at_first, at_second):
        value = jnp.where(left, first, second)
        value = jnp.where(special[0], at_first, value)
        return jnp.where(special[1], at_second, value).astype(f32)

    def turn(x):
        return pltpu.roll(x, HALF, 1)

    left_plus = jnp.where(left, 1.0, -1.0).astype(f32)
    to_x = (by_lane(1.0, 1.0, 1.0, 0.0), by_lane(-1.0, 1.0, 0.0, 1.0))
    to_y = (by_lane(1.0, 1.0, 0.0, 1.0), by_lane(1.0, -1.0, 1.0, 0.0))
    to_x_turned, to_y_turned = ([turn(v) for v in pair] for pair in (to_x, to_y))
    to_m = (by_lane(1.0, 1.0, 0.0, 1.0), by_lane(-1.0, -1.0, 1.0, 0.0))
    to_c = (by_lane(1.0, 1.0, 1.0, 0.0), by_lane(1.0, 1.0, 0.0, 0.0), by_lane(0.0, 0.0, 0.0, 1.0))
    to_s = (by_lane(1.0, -1.0, 1.0, 0.0), by_lane(0.0, 0.0, 0.0, -1.0))
    row_zero = iota((8, LANES), 0) == 0
    corner = row_zero & (lax.rem(iota((8, LANES), 1), HALF) == 0)
    lane_tall = iota((PATCH, LANES), 1)
    left_tall = lane_tall < HALF
    lag = iota((PATCH, 1), 0)
    lag = jnp.where(lag < PATCH // 2, lag, lag - PATCH).astype(f32)

    def at_row_zero(value, general):
        return jnp.concatenate([jnp.where(row_zero, value[:8], general[:8]), general[8:]], axis=0)

    def windows(v):
        first, second = v[:, :LANES], v[:, LANES:]
        return [
            jnp.where(lane_tall < LANES - RIM, first, 0.0),
            jnp.where(lane_tall < RIM, second, first),
            jnp.where(lane_tall < LANES - RIM, second, first),
            jnp.where(lane_tall < RIM, 0.0, second),
        ]

    def transform_rows(s, i, place, n):
        rows = pl.ds(pl.multiple_of(i * STRIDE, STRIDE), PATCH)
        window = jnp.concatenate([x_h[s, rows, :], x_l[s, rows, :]], axis=0)
        both = dot(table[0], window)
        for j, part in enumerate(windows(both[:PATCH] + both[PATCH:])):
            start = (n * 2 + j // 2) * PATCH
            y[place, j % 2, start : start + PATCH] = jnp.concatenate(split(part), axis=1)

    def spectra(place):
        both = [dot(y[place, k], table[1 + k]) for k in range(2)]
        both = [x[:, :LANES] + x[:, LANES:] for x in both]
        found = []
        for n in range(2):
            plain, turned = [], []
            for j in range(NODES):
                start = (n * 2 + j // 2) * PATCH
                c, d = both[j % 2][start : start + HALF], both[j % 2][start + HALF : start + PATCH]
                c_turned, d_turned = turn(c), turn(d)
                x_part = at_row_zero(c, c * to_x[0] + d_turned * to_x[1])
                y_part = at_row_zero(d * left_plus, c * to_y[0] + d_turned * to_y[1])
                plain.append(jnp.concatenate([x_part, y_part], axis=0))
                x_part = at_row_zero(c_turned, c_turned * to_x_turned[0] + d * to_x_turned[1])
                y_part = at_row_zero(-d_turned * left_plus, c_turned * to_y_turned[0] + d * to_y_turned[1])
                turned.append(jnp.concatenate([x_part, y_part], axis=0))
            found.append((plain, turned))
        return found

    def keep(ref, index, found):
        for n, parts in enumerate(found):
            for j, part in enumerate(parts):
                ref[index, n, j] = part

    def cross(first, second, j):
        a, a_turned = first[0, j], first[1, j]
        b, b_turned = second[0, j], second[1, j]
        whole = jnp.where(left_tall, a, a_turned) * b + jnp.where(left_tall, a_turned, -a) * b_turned
        alone = 0.5 * a * b
        x = jnp.concatenate([jnp.where(corner, alone[:8], whole[:8]), whole[8:HALF]], axis=0)
        low = whole[HALF:]
        z = jnp.concatenate([jnp.where(corner, alone[HALF : HALF + 8] * left_plus, low[:8]), low[8:]], axis=0)
        m = turn(x * to_m[0] + z * to_m[1])
        cosines = at_row_zero(x, x * to_c[0] + z * to_c[1] + m * to_c[2])
        sines = at_row_zero(z * left_plus, m * to_s[0] + z * to_s[1])
        return split(jnp.concatenate([cosines, sines], axis=0))

    def correlate(first, second):
        out = []
        for j in range(0, NODES, 2):
            parts = [cross(first, second, j + k) for k in range(2)]
            window = jnp.concatenate([jnp.concatenate([part[h] for part in parts], axis=1) for h in range(2)], axis=0)
            both = dot(table[3], window)
            high, low = split(both[:PATCH] + both[PATCH:])
            for k in range(2):
                lanes = slice(k * LANES, (k + 1) * LANES)
                out.append(jnp.concatenate([high[:, lanes], low[:, lanes]], axis=1))
        return out

    def pairs(earlier, rows, firsts, seconds):
        parts = [part for first, second in zip(firsts, seconds) for part in correlate(first, second)]
        both = dot(jnp.concatenate(parts, axis=0), table[4])
        both = both[:, :LANES] + both[:, LANES:]
        for n in range(NODES * len(rows)):
            i, j = rows[n // NODES], n % NODES
            scores = both[n * PATCH : (n + 1) * PATCH]
            top = jnp.max(scores, axis=0, keepdims=True)
            weights = jnp.exp2(scores - top)
            total = jnp.sum(weights, axis=0, keepdims=True)
            moment = jnp.sum(weights * lag, axis=0, keepdims=True)
            place = slice(j * LANES, (j + 1) * LANES)
            tops[i, pl.ds(earlier, 1), place] = top
            tops[i, pl.ds(earlier + SEC, 1), place] = top
            sums[i, pl.ds(earlier, 1), place] = total
            sums[i, pl.ds(earlier + SEC, 1), place] = moment

    def begin():
        pl.semaphore_wait(barrier, len(near))
        for copy in copies:
            copy.start()
        tell(0)

    lane8 = iota((8, LANES), 1)
    row8 = iota((8, LANES), 0)
    live = lax.rem(row8, SEC) + p > 0
    own_mask.wait()
    springs = jnp.zeros((8, LANES), f32)
    for i in range(NODES):
        here = jnp.concatenate([mask[s, i : i + 1, :] for s in range(SEC)], axis=0).astype(f32)
        here = jnp.concatenate([here, jnp.zeros((SEC, LANES - NODES), f32)], axis=1)
        here = jnp.concatenate([here, jnp.zeros((SEC, LANES), f32)], axis=0)
        springs = springs + (pltpu.roll(here, i * NODES, 1) if i else here)
    springs = jnp.where(live, springs, 0.0)

    def flat(x):
        return jnp.sum(pltpu.roll(x, 0, 1, stride=BLOCK, stride_axis=0), axis=0, keepdims=True)

    outbox[0, 1:2, :] = flat(springs)
    own.wait()
    for s in range(1, SEC + 1):
        prepare(s, RIM, ROWS)
    begin()
    first_tables.wait()
    for s in range(1, SEC + 1):
        for n in range(2):
            transform_rows(s, 1 + n, s, n)
    other_tables.wait()

    @pl.loop(0, 2)
    def _(outer):
        rows = (1 - outer, 2 + outer)

        @pl.when(outer == 1)
        def _():
            hear(0)
            tell(1)
            for copy in copies[4:]:
                copy.wait_recv()
            for s in range(1, SEC + 1):
                prepare_top(s)
                prepare_bottom(s)
            for s in range(1, SEC + 1):
                for n in range(2):
                    transform_rows(s, 3 * n, s, n)

        for s in range(1, SEC + 1):
            for n, parts in enumerate(spectra(s)):
                if s == 1:
                    keep(first_spec, rows[n], parts)
                keep(spec, (s - 1) * 2 + n, parts)
            if s > 1:
                pairs(s - 1, rows, [spec.at[(s - 2) * 2 + n] for n in range(2)], [spec.at[(s - 1) * 2 + n] for n in range(2)])

    hear(1)
    tell(2)
    for n in range(2):
        for copy in copies[2 * n : 2 * n + 2]:
            copy.wait_recv()
        if n == 0:
            prepare_top(0)
            prepare(0, RIM, SPLIT)
        else:
            prepare(0, RIM + SPLIT, ROWS - SPLIT)
            prepare_bottom(0)
        rows = (2 * n, 2 * n + 1)
        for k in range(2):
            transform_rows(0, rows[k], n, k)
        for k, parts in enumerate(spectra(n)):
            keep(spec, rows[k], parts)
        pairs(0, rows, [spec.at[i] for i in rows], [first_spec.at[i] for i in rows])

    lag_cols = jnp.where(lane8 < PATCH // 2, lane8, lane8 - PATCH).astype(f32)
    along = jnp.zeros((8, LANES), f32)
    across = jnp.zeros((8, LANES), f32)
    for i in range(NODES):
        for j in range(NODES):
            lanes = slice(j * LANES, (j + 1) * LANES)
            top = tops[i, :, lanes]
            scaled = sums[i, :, lanes] * jnp.exp2(top - jnp.max(top, axis=1, keepdims=True))
            here = lane8 == i * NODES + j
            along = jnp.where(here, jnp.sum(scaled, axis=1, keepdims=True), along)
            across = jnp.where(here, jnp.sum(scaled * lag_cols, axis=1, keepdims=True), across)
    low_half = row8 < SEC
    numerator = jnp.where(low_half, pltpu.roll(along, SEC, 0), pltpu.roll(across, SEC, 0))
    denominator = jnp.where(low_half, along, pltpu.roll(along, SEC, 0))
    flows = jnp.where(live & (lane8 < BLOCK), numerator / denominator, 0.0)

    outbox[0, 0:1, :] = flat(flows)
    inbox[(1 + px) * tiles + t] = outbox[0]

    def give(q, sem, device):
        return remote(outbox, inbox.at[pl.ds(q * tiles + t, 1)], flow_send.at[sem], flow_recv, device)

    def whole(ref, count, sem):
        slots = ref.at[pl.ds(0, count)]
        pltpu.make_async_copy(slots, slots, sem).wait()

    def write(out, x):
        for i in range(NODES):
            moved = pltpu.roll(x, LANES - i * NODES, 1) if i else x
            for c in range(2):
                for s in range(SEC):
                    out[c, s, i : i + 1, :] = moved[c * SEC + s : c * SEC + s + 1, :NODES]

    for device in plane_mates:
        give(1 + px, 0, device).start()

    @pl.when(at_high)
    def _():
        for x in range(X_COUNT):
            for n in range(tiles):
                give(0, 1, (z_next * X_COUNT + x, n)).start()

    @pl.when(at_low)
    def _():
        for x in range(X_COUNT):
            for n in range(tiles):
                give(X_COUNT + 1, 1, (z_back * X_COUNT + x, n)).start()


    write(flow_out, flows)

    whole(inbox, plane - 1 + 2 * tiles, flow_recv)

    block = lax.div(lane8, BLOCK)

    def transpose_blocks(x):
        for bit in (1, 2, 4):
            row_bit, lane_bit = (row8 & bit) > 0, (block & bit) > 0
            up = pltpu.roll(pltpu.roll(x, 8 - bit, 0), BLOCK * bit, 1)
            down = pltpu.roll(pltpu.roll(x, bit, 0), LANES - BLOCK * bit, 1)
            x = jnp.where(row_bit == lane_bit, x, jnp.where(row_bit, down, up))
        return x

    def received(q, row):
        x = inbox[q * tiles : (q + 1) * tiles, row, :]
        if tiles < 8:
            x = jnp.concatenate([x, jnp.zeros((8 - tiles, LANES), f32)], axis=0)
        if q == 0:
            x = x * (pz > 0).astype(f32)
        elif q == X_COUNT + 1:
            x = x * (pz < z_count - 1).astype(f32)
        return x

    flow_parts, spring_parts = ([], []), []
    left8 = lane8 < HALF
    for q in range(0, X_COUNT + 2, 2):
        first, second = received(q, 0), received(q + 1, 0)
        flow_parts[0].append(transpose_blocks(jnp.where(left8, first, pltpu.roll(second, HALF, 1))))
        flow_parts[1].append(transpose_blocks(jnp.where(left8, pltpu.roll(first, HALF, 1), second)))
        spring_parts.append(transpose_blocks(received(q, 1) + pltpu.roll(received(q + 1, 1), HALF, 1)))
    wide = (X_COUNT + 2) * SEC
    spring = jnp.concatenate(spring_parts, axis=0)
    flow = [jnp.concatenate(parts, axis=0) for parts in flow_parts]
    lane = iota((wide, LANES), 1)
    node_col = lax.rem(lane, NODES)
    live_lanes = (lane < tiles * BLOCK).astype(f32)
    has_up, has_down = (lane >= NODES).astype(f32), (lane < LANES - NODES).astype(f32)
    has_left, has_right = (node_col > 0).astype(f32), (node_col < NODES - 1).astype(f32)

    def differ(stretch):
        return inter_stiff * (pltpu.roll(stretch, wide - 1, 0) - stretch)

    def apply(v):
        stretch = spring * (v - pltpu.roll(v, 1, 0))
        beside = (
            has_up * pltpu.roll(v, NODES, 1)
            + has_down * pltpu.roll(v, LANES - NODES, 1)
            + has_left * pltpu.roll(v, 1, 1)
            + has_right * pltpu.roll(v, LANES - 1, 1)
        )
        return live_lanes * (differ(stretch) + plane_stiff * (beside - 4.0 * v))

    powers = []
    for c in range(2):
        chain = [differ(-spring * flow[c])]
        for _ in range(STEPS - 1):
            chain.append(apply(chain[-1]))
        powers.append(chain)
    grams = [(a, b) for a in range(STEPS) for b in range(a, STEPS)]
    row = iota((wide, LANES), 0)
    inner = ((row >= SEC) & (row < wide - SEC)).astype(f32)
    inner_powers = [[v * inner for v in chain] for chain in powers]
    rows = [
        jnp.sum(inner_powers[0][a] * powers[0][b] + inner_powers[1][a] * powers[1][b], axis=0, keepdims=True)
        for a, b in grams
    ]
    totals = jnp.concatenate(rows + [jnp.zeros((16 - len(grams), LANES), f32)], axis=0)
    totals = jnp.sum(totals, axis=1, keepdims=True)
    diagonal = iota((16, LANES), 0) == iota((16, LANES), 1)
    plane_sum[0] = jnp.sum(jnp.where(diagonal, totals, 0.0), axis=0, keepdims=True)

    def to_z(n):
        slot = pl.ds(n, 1)
        return remote(plane_sum.at[pl.ds(0, 1)], plane_sum.at[slot], sum_send, sum_recv, z_by_step[n])

    hear(2)
    for n in sorted(range(1, z_count), key=lambda n: -hops(n, z_count)):
        to_z(n).start()

    mine = []
    for a in range(STEPS):
        both = jnp.zeros((8, LANES), f32)
        for q in range(X_COUNT):
            part = slice(SEC + q * SEC, 2 * SEC + q * SEC)
            here = jnp.concatenate([powers[0][a][part], powers[1][a][part]], axis=0)
            both = jnp.where(px == q, here, both)
        mine.append(pltpu.roll(both, lax.rem(LANES - t * BLOCK, LANES), 1))

    for copy in copies:
        copy.wait_send()

    whole(inbox, plane - 1, flow_send.at[0])

    @pl.when(at_low | at_high)
    def _():
        whole(inbox, plane, flow_send.at[1])

    whole(plane_sum, z_count - 1, sum_recv)

    totals = jnp.sum(plane_sum[0:z_count, 0, :], axis=0, keepdims=True)
    gram = {}
    for n, (a, b) in enumerate(grams):
        gram[a, b] = gram[b, a] = totals[:, n : n + 1]
    count = 2 * SEC * NODES * NODES * slabs * tiles
    zero = jnp.zeros((1, 1), f32)
    force = [zero + 1.0, zero, zero, zero]
    moved = [zero] * STEPS
    for step in range(STEPS):
        square = zero
        for a in range(step + 1):
            square = square + force[a] * force[a] * gram[a, a]
            for b in range(a + 1, step + 1):
                square = square + 2.0 * force[a] * force[b] * gram[a, b]
        scale = step_size / jnp.sqrt(jnp.maximum(square, 0.0) / count + norm_eps)
        moved = [m + scale * f for m, f in zip(moved, force)]
        force = [f + (scale * force[n - 1] if n else 0.0) for n, f in enumerate(force)]
    write(mesh_out, sum(m * v for m, v in zip(moved, mine)))
    whole(plane_sum, z_count - 1, sum_send)


def local(slabs, tiles, images, tissue_mask):
    z_count = max(slabs // X_COUNT, 1)
    plane = X_COUNT * tiles
    vmem = pl.BlockSpec(memory_space=pltpu.VMEM)
    hbm = pl.BlockSpec(memory_space=pltpu.HBM)
    constants = jnp.asarray(tables())
    out = jax.ShapeDtypeStruct((2, SEC, NODES, NODES), f32)
    dma = pltpu.SemaphoreType.DMA
    return pl.pallas_call(
        functools.partial(kernel, slabs, tiles),
        out_shape=(out, out),
        in_specs=[hbm, hbm, hbm],
        out_specs=(vmem, vmem),
        scratch_shapes=[
            pltpu.VMEM((SEC + 1, WIDE, COLS), f32),
            pltpu.VMEM((SEC, NODES, NODES), jnp.int32),
            pltpu.VMEM(constants.shape, bf16),
            pltpu.VMEM((SEC + 1, WIDE, COLS), bf16),
            pltpu.VMEM((SEC + 1, WIDE, COLS), bf16),
            pltpu.VMEM((SEC + 1, 2, NODES * PATCH, COLS), bf16),
            pltpu.VMEM((2 * SEC, 2, NODES, PATCH, LANES), f32),
            pltpu.VMEM((NODES, 2, NODES, PATCH, LANES), f32),
            pltpu.VMEM((NODES, 2 * SEC, NODES * LANES), f32),
            pltpu.VMEM((NODES, 2 * SEC, NODES * LANES), f32),
            pltpu.VMEM((1, 2, LANES), f32),
            pltpu.VMEM(((X_COUNT + 2) * tiles, 2, LANES), f32),
            pltpu.VMEM((z_count, 1, LANES), f32),
            dma((4,)),
            dma((6,)),
            dma((6,)),
            dma((2,)),
            dma,
            dma,
            dma,
            pltpu.SemaphoreType.REGULAR((3,)),
        ],
        compiler_params=pltpu.CompilerParams(
            collective_id=0, has_side_effects=True, vmem_limit_bytes=64 * 1024 * 1024 - 65536
        ),
    )(images, tissue_mask, constants)


def solution(mesh):
    placed = (P("slab", "tile", None), P("slab", "tile", None))
    return jax.shard_map(
        functools.partial(local, mesh.shape["slab"], mesh.shape["tile"]),
        mesh=mesh,
        in_specs=placed,
        out_specs=(P(None, "slab", "tile", None), P(None, "slab", "tile", None)),
        check_vma=False,
    )
```
